32 devices in a mesh: parts: 2 (over x), date: 16 (over z, y, core).
Axes of the slice: x: 2, y: 2, z: 4, core: 2. Of those that a mesh axis runs over, the one named last changes fastest.
Arguments:
- slave_acquisitions: bfloat16 [32, 2, 192, 2112], P(('parts', 'date')), parts along dimension 0, may hold values from -6 to 6
- master_subswath_crop: bfloat16 [2, 256, 2048], P(None, 'parts', 'date'), parts along dimension 1, may hold values from -6 to 6
- deskew_angular_slope: float32 [2048], P('date'), may hold values from 4 to 40
- deskew_central_epoch: float32 [2048], P('date'), may hold values from 0.2 to 0.8
- along_track_whole_row: int32 [32, 128], P(('parts', 'date')), parts along dimension 0, may hold values from 3 to 134, as said below
- along_track_subpixel: float32 [32, 128], P(('parts', 'date')), parts along dimension 0, may hold values from 0 to 1
- along_track_strip_opening: int32 [32, 1], P(('parts', 'date')), parts along dimension 0, may hold values from 0 to 0
- slant_whole_column: int32 [32, 2048], P(('parts', 'date')), parts along dimension 0, may hold values from 3 to 2054, as said below
- slant_subpixel: float32 [32, 2048], P(('parts', 'date')), parts along dimension 0, may hold values from 0 to 1
- slant_strip_opening: int32 [32, 16], P(('parts', 'date')), parts along dimension 0, may hold values from 0 to 1920
Outputs:
- interferogram: float32 [32, 2, 32, 128], P(('parts', 'date')), parts along dimension 0
- stack_power: float32 [64, 128], P('parts'), parts along dimension 0
The draws below stay inside these ranges and needn't reach their ends.
There are 2 independent parts, one for each index of `parts`. The reference program is written for one: setup_inputs(seed, part) draws one part's arguments, and reference() takes and returns one part's arrays. A program takes and returns all parts, laid end to end along the dimension named above; an argument that names none is the same for every part. Nothing has to cross between parts.
Inputs may be any that keep to these rules, and one draw needn't show every extreme that they name: For every date and every output line i of block b = i // 128, the lines along_track_whole_row - 3 to along_track_whole_row + 4 lie within along_track_strip_opening[b] to along_track_strip_opening[b] + 191. For every date and every output sample c of block b = c // 128, the samples slant_whole_column - 3 to slant_whole_column + 4 lie within slant_strip_opening[b] to slant_strip_opening[b] + 191.
All inputs are finite; a program needn't handle non-finite values.
Results may differ from the reference program's by a relative error of at most 0.0051.
Values may be sent and summed in bfloat16 or wider, within the bound.
A program may use at most 128 MiB of HBM per device.

```python
import math
import jax
import jax.numpy as jnp
from jax import lax

ALONG_TRACK_ROWS = 128
TAPS = 8
BLK = 128
WIN = 192
MARGIN = 64
LOOK_AZ = 4
LOOK_RG = 16
DATES = 16
SLANT_COLUMNS = 2048
AZ_IN = 192
RG_IN = 2112


def band_draw(key, length, salt):
    base_key = jax.random.fold_in(key, salt)
    span_extra = MARGIN - WIN + BLK
    slack_cells = WIN - BLK - TAPS - 3
    reach_low = TAPS // 2 + 1
    offsets = jax.random.randint(jax.random.fold_in(base_key, 1), (DATES,), reach_low, reach_low + span_extra + 1)
    offsets = offsets.at[0].set(reach_low).at[1].set(reach_low + span_extra)
    wobble = jax.random.randint(jax.random.fold_in(base_key, 2), (DATES, length), -2, 3)
    wobble = wobble.at[0, 0].set(-2).at[1, length - 1].set(2)
    positions = jnp.arange(length, dtype=jnp.int32)[None, :] + offsets[:, None] + wobble
    block_count = length // BLK
    base_start = jnp.arange(block_count, dtype=jnp.int32)[None, :] * BLK + offsets[:, None] - reach_low
    upper_bound = jnp.minimum(slack_cells, base_start)
    backstep = jax.random.randint(jax.random.fold_in(base_key, 3), (DATES, block_count), 0, upper_bound + 1)
    backstep = backstep.at[1, block_count - 1].set(0)
    return (positions.astype(jnp.int32), (base_start - backstep).astype(jnp.int32))


def draw_along_track_whole_row(key, part):
    positions, starts = band_draw(key, ALONG_TRACK_ROWS, 11)
    return positions


def draw_along_track_strip_opening(key, part):
    positions, starts = band_draw(key, ALONG_TRACK_ROWS, 11)
    return starts


def draw_slant_whole_column(key, part):
    positions, starts = band_draw(key, SLANT_COLUMNS, 23)
    return positions


def draw_slant_strip_opening(key, part):
    positions, starts = band_draw(key, SLANT_COLUMNS, 23)
    return starts


def steps_of(key, shape, cuts, smallest, largest):
    factor_of, own = 1.0, jax.random.fold_in(key, 6)
    for dim, blocks in cuts:
        heights = jnp.exp(jax.random.uniform(jax.random.fold_in(own, dim), (blocks,), jnp.float32, smallest / len(cuts), largest / len(cuts)))
        factor_of = factor_of * jnp.repeat(heights, shape[dim] // blocks).reshape([-1 if axis == dim else 1 for axis in range(len(shape))])
    return factor_of


def centred(key, shape, deviation, most, cuts=(), held_as=jnp.bfloat16):
    loudness = steps_of(key, shape, cuts, -0.22, 0.18) if cuts else 1.0
    drawn = jax.random.normal(key, shape, jnp.float32) * deviation * loudness
    return jnp.minimum(jnp.maximum(drawn, -most), most).astype(held_as)


def setup_inputs(seed: int = 0, part: int = 0) -> dict:
    seeds = jax.random.split(jax.random.key(seed), 11)
    own_keys = jax.random.split(jax.random.fold_in(seeds[10], part), 11)
    return {
        "slave_acquisitions": centred(own_keys[0], (DATES, 2, AZ_IN, RG_IN), 1.0, 6.0, ((0, 16),)),
        "master_subswath_crop": centred(own_keys[1], (2, ALONG_TRACK_ROWS, SLANT_COLUMNS), 1.0, 6.0, ((2, 16),)),
        "deskew_angular_slope": jnp.clip(jnp.exp(math.log(40.0) - 2.3025851 * jax.random.uniform(seeds[2], (SLANT_COLUMNS,), jnp.float32) ** steps_of(seeds[2], (SLANT_COLUMNS,), ((0, 16),), -0.2, 0.2)), 4.0, 40.0),
        "deskew_central_epoch": jnp.clip(0.2 + 0.6 * jax.random.uniform(seeds[3], (SLANT_COLUMNS,), jnp.float32) ** steps_of(seeds[3], (SLANT_COLUMNS,), ((0, 16),), -0.2, 0.2), 0.2, 0.8),
        "along_track_whole_row": draw_along_track_whole_row(jax.random.fold_in(jax.random.fold_in(seeds[10], part), 71), part),
        "along_track_subpixel": jnp.clip(1.0 * jax.random.uniform(own_keys[5], (DATES, ALONG_TRACK_ROWS), jnp.float32) ** steps_of(own_keys[5], (DATES, ALONG_TRACK_ROWS), ((0, 16),), -0.2, 0.2), 0.0, 1.0),
        "along_track_strip_opening": draw_along_track_strip_opening(jax.random.fold_in(jax.random.fold_in(seeds[10], part), 71), part),
        "slant_whole_column": draw_slant_whole_column(jax.random.fold_in(jax.random.fold_in(seeds[10], part), 71), part),
        "slant_subpixel": jnp.clip(1.0 * jax.random.uniform(own_keys[8], (DATES, SLANT_COLUMNS), jnp.float32) ** steps_of(own_keys[8], (DATES, SLANT_COLUMNS), ((0, 16),), -0.2, 0.2), 0.0, 1.0),
        "slant_strip_opening": draw_slant_strip_opening(jax.random.fold_in(jax.random.fold_in(seeds[10], part), 71), part),
    }


epsilon = 1e-06

def kernel_weights(fraction):
    tap_offsets = jnp.arange(TAPS, dtype=jnp.float32) - (TAPS // 2 - 1)
    spacing = tap_offsets[None, :] - fraction[:, None]
    return jnp.sinc(spacing) * (0.5 + 0.5 * jnp.cos(jnp.pi * spacing / (TAPS // 2)))

def tap_block(positions, weights, first_cell):
    tap_steps = jnp.arange(TAPS, dtype=jnp.int32) - (TAPS // 2 - 1)
    target = positions[:, None] + tap_steps[None, :] - first_cell
    window_cells = jnp.arange(WIN, dtype=jnp.int32)
    matches = (target[:, :, None] == window_cells[None, None, :]).astype(jnp.float32)
    return lax.optimization_barrier(jnp.sum(weights[:, :, None] * matches, axis=1)).astype(jnp.bfloat16)

def looks_mean(values):
    leading = values.shape[:-2]
    shaped = values.reshape(leading + (values.shape[-2] // LOOK_AZ, LOOK_AZ, values.shape[-1] // LOOK_RG, LOOK_RG))
    return shaped.mean(axis=(-3, -1))

def coregister(second_date, row_pos, row_frac, row_band, col_pos, col_frac, col_band, deskew_angular_slope, deskew_central_epoch):
    lines_in = second_date.shape[1]
    line_time = jnp.arange(lines_in, dtype=jnp.float32) / lines_in
    range_weights = kernel_weights(col_frac)

    def range_step(block_index):
        first_cell = col_band[block_index]
        window = lax.dynamic_slice_in_dim(second_date, first_cell, WIN, 2)
        columns = lax.dynamic_slice_in_dim(col_pos, block_index * BLK, BLK)
        weights = lax.dynamic_slice_in_dim(range_weights, block_index * BLK, BLK, 0)
        tap_matrix = tap_block(columns, weights, first_cell)
        ranged = jnp.einsum('pjw,cw->pjc', window.astype(jnp.float32), tap_matrix.astype(jnp.float32))
        rate_block = lax.dynamic_slice_in_dim(deskew_angular_slope, block_index * BLK, BLK)
        center_block = lax.dynamic_slice_in_dim(deskew_central_epoch, block_index * BLK, BLK)
        offsets = line_time[:, None] - center_block[None, :]
        phases = rate_block[None, :] * offsets * offsets
        cosine = jnp.cos(phases)
        sine_part = jnp.sin(phases)
        real_part = ranged[0] * cosine + ranged[1] * sine_part
        imag_part = ranged[1] * cosine - ranged[0] * sine_part
        return jnp.stack([real_part, imag_part]).astype(jnp.bfloat16)
    blocks = lax.map(range_step, jnp.arange(SLANT_COLUMNS // BLK, dtype=jnp.int32))
    deramped = jnp.transpose(blocks, (1, 2, 0, 3)).reshape(2, lines_in, SLANT_COLUMNS)
    azimuth_weights = kernel_weights(row_frac)
    position = row_pos.astype(jnp.float32) + row_frac

    def azimuth_step(block_index):
        first_cell = row_band[block_index]
        window = lax.dynamic_slice_in_dim(deramped, first_cell, WIN, 1)
        row_positions = lax.dynamic_slice_in_dim(row_pos, block_index * BLK, BLK)
        weights = lax.dynamic_slice_in_dim(azimuth_weights, block_index * BLK, BLK, 0)
        tap_matrix = tap_block(row_positions, weights, first_cell)
        moved = jnp.einsum('iw,pwc->pic', tap_matrix.astype(jnp.float32), window.astype(jnp.float32))
        place_time = lax.dynamic_slice_in_dim(position, block_index * BLK, BLK) / lines_in
        offsets = place_time[:, None] - deskew_central_epoch[None, :]
        phases = deskew_angular_slope[None, :] * offsets * offsets
        cosine = jnp.cos(phases)
        sine_part = jnp.sin(phases)
        real_part = moved[0] * cosine - moved[1] * sine_part
        imag_part = moved[0] * sine_part + moved[1] * cosine
        return jnp.stack([real_part, imag_part]).astype(jnp.bfloat16)
    blocks = lax.map(azimuth_step, jnp.arange(ALONG_TRACK_ROWS // BLK, dtype=jnp.int32))
    return jnp.transpose(blocks, (1, 0, 2, 3)).reshape(2, ALONG_TRACK_ROWS, SLANT_COLUMNS)

def reference(slave_acquisitions, master_subswath_crop, deskew_angular_slope, deskew_central_epoch, along_track_whole_row, along_track_subpixel, along_track_strip_opening, slant_whole_column, slant_subpixel, slant_strip_opening):
    master_pixel_values = master_subswath_crop.astype(jnp.float32)
    ref_power = looks_mean(master_pixel_values[0] * master_pixel_values[0] + master_pixel_values[1] * master_pixel_values[1])

    def per_date(inputs):
        second_date, row_pos, row_frac, row_band, col_pos, col_frac, col_band = inputs
        resampled = coregister(second_date, row_pos, row_frac, row_band, col_pos, col_frac, col_band, deskew_angular_slope, deskew_central_epoch)
        sec_values = resampled.astype(jnp.float32)
        real_part = master_pixel_values[0] * sec_values[0] + master_pixel_values[1] * sec_values[1]
        imag_part = master_pixel_values[1] * sec_values[0] - master_pixel_values[0] * sec_values[1]
        sec_power = looks_mean(sec_values[0] * sec_values[0] + sec_values[1] * sec_values[1])
        normalizer = 1.0 / jnp.sqrt(ref_power * sec_power + epsilon)
        return (jnp.stack([looks_mean(real_part) * normalizer, looks_mean(imag_part) * normalizer]), sec_power)
    interferogram, powers = lax.map(per_date, (slave_acquisitions, along_track_whole_row, along_track_subpixel, along_track_strip_opening, slant_whole_column, slant_subpixel, slant_strip_opening))
    stack_power = lax.optimization_barrier(jnp.sum(powers, axis=0)) / DATES
    return (interferogram, stack_power)
```

```python
import functools
import math

import jax
import jax.numpy as jnp
from jax import lax
from jax.experimental import pallas as pl
from jax.experimental.pallas import tpu as pltpu
from jax.sharding import PartitionSpec as P

TAPS = 8
LEAD = TAPS // 2 - 1
BLK = 128
WIN = 192
LOOK_AZ = 4
LOOK_RG = 16
HALF = 64
EPSILON = 1e-06
MESH = pl.DeviceIdType.MESH
SIN_TERMS = (4.442882919124343, -7.308245686509025, 3.6063542184321515, -0.8461116503693629, 0.10982451641673696)
COS_TERMS = (1.414213496255228, -6.978850948563791, 5.739460376906791, -1.8835579059844396, 0.3106880275224321)


def poly(terms, x):
    total = jnp.full_like(x, terms[-1])
    for term in terms[-2::-1]:
        total = total * x + term
    return total


def sincos_turns(turns):
    rest = turns - jnp.round(turns)
    square = rest * rest
    sine = rest * poly(SIN_TERMS, square)
    cosine = poly(COS_TERMS, square)
    return sine * cosine, 1.0 - sine * sine


def tap_weights(fraction):
    step = lax.broadcasted_iota(jnp.int32, (TAPS, fraction.shape[1]), 0) - LEAD
    spacing = step.astype(jnp.float32) - fraction
    angle = math.pi * spacing
    sine, _ = sincos_turns(spacing * 0.5)
    sinc = jnp.where(spacing == 0.0, 1.0, sine / jnp.where(spacing == 0.0, 1.0, angle))
    _, cosine = sincos_turns(spacing * 0.125)
    return sinc * (0.5 + 0.5 * cosine)


def tap_matrix(first, weights, cells):
    cell = lax.broadcasted_iota(jnp.int32, (cells, first.shape[1]), 0) - first
    total = jnp.zeros(cell.shape, jnp.float32)
    for k in range(TAPS):
        total = jnp.where(cell == k, weights[k : k + 1], total)
    return total.astype(jnp.bfloat16)


def slab_sum(values):
    rows = values.shape[0] // LOOK_AZ
    total = values[:rows]
    for b in range(1, LOOK_AZ):
        total = total + values[b * rows : (b + 1) * rows]
    return total


def looked(values, gather):
    high = values.astype(jnp.bfloat16)
    low = (values - high.astype(jnp.float32)).astype(jnp.bfloat16)
    return jnp.dot(jnp.concatenate([high, low], axis=1), gather, preferred_element_type=jnp.float32)


def kernel(
    parties,
    x_hbm, master_ref, rate_ref, center_ref, row_pos, row_frac, col_pos, col_frac, col_band,
    ifg_ref, stack_ref,
    x0, xs, weights, own_rc, rc, mg, res, times, place, acc, acc_sec, chunks, parts, totals,
    in_sems, rc_s, rc_r, m_s, m_r, p_s, p_r, t_s, t_r,
):
    me = lax.axis_index("date")
    lines_in = x0.shape[1]
    tiles_in = xs.shape[0] // 2
    last_half = xs.shape[0] - 3
    blocks = col_pos.shape[1] // BLK
    rows_out = row_pos.shape[1]
    looks_out = rows_out // LOOK_AZ
    per_tile = BLK * LOOK_RG // BLK

    fetch0 = pltpu.make_async_copy(x_hbm.at[0], x0, in_sems.at[0])
    fetch0.start()

    def tile_copy(t):
        lanes = pl.ds(pl.multiple_of(t * BLK, BLK), BLK)
        return pltpu.make_async_copy(x_hbm.at[0, :, :, lanes], xs.at[2 * t], in_sems.at[t + 1])

    def tile_start(t, _):
        tile_copy(t).start()
        return 0

    def tile_wait(t, _):
        tile_copy(t).wait()
        return 0

    lax.fori_loop(0, tiles_in, tile_start, 0)

    barrier = pltpu.get_barrier_semaphore()

    def greet(s, _):
        pl.semaphore_signal(barrier, inc=1, device_id={"date": lax.rem(me + s, parties)}, device_id_type=MESH)
        return 0

    lax.fori_loop(1, parties, greet, 0)

    own_rc[...] = jnp.zeros_like(own_rc)
    own_rc[0:1, :] = rate_ref[...] * (0.5 / math.pi)
    own_rc[1:2, :] = center_ref[...]
    rc[pl.ds(me, 1)] = own_rc[...][None]
    to = lax.broadcasted_iota(jnp.int32, (rows_out, rows_out), 0)
    source = lax.broadcasted_iota(jnp.int32, (rows_out, rows_out), 1)
    order = jnp.where(source == LOOK_AZ * (to % looks_out) + to // looks_out, 1.0, 0.0).astype(jnp.bfloat16)
    for p in range(2):
        mg[pl.ds(me, 1), p] = jnp.dot(order, master_ref[p], preferred_element_type=jnp.float32).astype(jnp.bfloat16)[None]

    pl.semaphore_wait(barrier, parties - 1)

    def rc_copy(slot, peer):
        return pltpu.make_async_remote_copy(
            src_ref=own_rc, dst_ref=rc.at[slot], send_sem=rc_s.at[peer], recv_sem=rc_r.at[slot],
            device_id={"date": peer}, device_id_type=MESH)

    def rc_send(s, _):
        rc_copy(me, lax.rem(me + s, parties)).start()
        return 0

    lax.fori_loop(1, parties, rc_send, 0)

    deep = parties // 4
    my_z, my_y, my_c = me // 4, (me // 2) % 2, me % 2
    across = my_z * 4 + (1 - my_y) * 2 + my_c
    twin = my_z * 4 + my_y * 2 + (1 - my_c)

    def m_copy(slot, peer, kind, tag):
        return pltpu.make_async_remote_copy(
            src_ref=mg.at[slot], dst_ref=mg.at[slot], send_sem=m_s.at[kind, tag], recv_sem=m_r.at[slot],
            device_id={"date": peer}, device_id_type=MESH)

    def z_index(s):
        return lax.rem(my_z + s, deep) * 4

    def z_send(s, _):
        peer = z_index(s) + my_y * 2 + my_c
        m_copy(me, peer, 0, peer).start()
        return 0

    m_copy(me, across, 1, me).start()
    lax.fori_loop(1, deep, z_send, 0)
    m_copy(me, twin, 2, me).start()

    def z_pass(s, _):
        slot = z_index(s) + my_y * 2 + my_c
        m_copy(slot, slot, 0, slot).wait_recv()
        m_copy(slot, across, 1, slot).start()
        m_copy(slot, twin, 2, slot).start()
        return 0

    def y_pass(s, _):
        slot = z_index(s) + (1 - my_y) * 2 + my_c
        m_copy(slot, across, 1, slot).wait_recv()
        m_copy(slot, twin, 2, slot).start()
        return 0

    def twin_wait(s, _):
        for y in range(2):
            slot = z_index(s) + y * 2 + (1 - my_c)
            m_copy(slot, twin, 2, slot).wait_recv()
        return 0

    weights[...] = tap_weights(col_frac[...])
    row_taps = tap_matrix(row_pos[...] - LEAD, tap_weights(row_frac[...]), lines_in)
    row_taps = lax.dot_general(
        order, row_taps, (((1,), (1,)), ((), ())), preferred_element_type=jnp.float32
    ).astype(jnp.bfloat16)
    when = (row_pos[...].astype(jnp.float32) + row_frac[...]) / lines_in
    times[...] = jnp.transpose(jnp.broadcast_to(when, (BLK, rows_out)))
    for b in range(LOOK_AZ):
        place[b * looks_out : (b + 1) * looks_out, :] = times[pl.ds(b, looks_out, stride=LOOK_AZ), :]
    lane = lax.broadcasted_iota(jnp.int32, (2 * BLK, BLK), 0) % BLK
    out_lane = lax.broadcasted_iota(jnp.int32, (2 * BLK, BLK), 1)
    gather = jnp.where(lane // LOOK_RG == out_lane, 1.0, 0.0).astype(jnp.bfloat16)
    acc[...] = jnp.zeros_like(acc)
    acc_sec[...] = jnp.zeros_like(acc_sec)

    fetch0.wait()
    lax.fori_loop(0, tiles_in, tile_wait, 0)
    for t in range(tiles_in):
        xs[2 * t + 1] = x0[:, :, t * BLK + HALF : (t + 1) * BLK + HALF]

    def rc_wait(s, _):
        slot = lax.rem(me + s, parties)
        rc_copy(slot, slot).wait_recv()
        return 0

    lax.fori_loop(1, parties, rc_wait, 0)

    line_time = lax.broadcasted_iota(jnp.int32, (lines_in, BLK), 0).astype(jnp.float32) / lines_in

    def resample(b, _):
        half = lax.min(lax.div(col_band[0, b], HALF), last_half)
        window = jnp.concatenate([xs[half], xs[half + 2]], axis=2).reshape(2 * lines_in, 2 * BLK)
        columns = pl.ds(pl.multiple_of(b * BLK, BLK), BLK)
        taps = tap_matrix(col_pos[:, columns] - (LEAD + HALF * half), weights[:, columns], 2 * BLK)
        ranged = jnp.dot(window, taps, preferred_element_type=jnp.float32)
        rate, center = rc[b, 0:1, :], rc[b, 1:2, :]
        offset = line_time - center
        sine, cosine = sincos_turns(rate * offset * offset)
        real, imag = ranged[:lines_in], ranged[lines_in:]
        deramped = jnp.concatenate(
            [(real * cosine + imag * sine).astype(jnp.bfloat16), (imag * cosine - real * sine).astype(jnp.bfloat16)],
            axis=1)
        moved = jnp.dot(row_taps, deramped, preferred_element_type=jnp.float32)
        offset = place[...] - center
        sine, cosine = sincos_turns(rate * offset * offset)
        real, imag = moved[:, :BLK], moved[:, BLK:]
        real, imag = (
            (real * cosine - imag * sine).astype(jnp.bfloat16),
            (real * sine + imag * cosine).astype(jnp.bfloat16),
        )
        res[b, 0] = real
        res[b, 1] = imag
        real, imag = real.astype(jnp.float32), imag.astype(jnp.float32)
        sums = looked(slab_sum(real * real + imag * imag), gather)
        acc_sec[b // per_tile] += pltpu.roll(sums, (b % per_tile) * (BLK // LOOK_RG), 1)
        return 0

    cut = blocks // 2
    lax.fori_loop(0, cut, resample, 0)
    lax.fori_loop(1, deep, z_pass, 0)
    lax.fori_loop(cut, blocks, resample, 0)
    lax.fori_loop(0, deep, y_pass, 0)

    per_slab = looks_out // 2
    scale = 1.0 / (LOOK_AZ * LOOK_RG)
    for d in range(parties):
        chunks[d] = acc_sec[d // per_slab, 2 * (d % per_slab) : 2 * (d % per_slab) + 2, :]

    def p_copy(chunk, slot, peer):
        return pltpu.make_async_remote_copy(
            src_ref=chunks.at[chunk], dst_ref=parts.at[slot], send_sem=p_s.at[peer], recv_sem=p_r.at[slot],
            device_id={"date": peer}, device_id_type=MESH)

    def p_send(s, _):
        peer = lax.rem(me + s, parties)
        p_copy(peer, me, peer).start()
        return 0

    lax.fori_loop(1, parties, p_send, 0)
    parts[pl.ds(me, 1)] = chunks[pl.ds(me, 1)]

    lax.fori_loop(0, deep, twin_wait, 0)

    def combine(b, _):
        m0, m1 = mg[b, 0].astype(jnp.float32), mg[b, 1].astype(jnp.float32)
        r0, r1 = res[b, 0].astype(jnp.float32), res[b, 1].astype(jnp.float32)
        rows = jnp.concatenate(
            [slab_sum(m0 * r0 + m1 * r1), slab_sum(m1 * r0 - m0 * r1), slab_sum(m0 * m0 + m1 * m1)], axis=0)
        sums = looked(rows, gather)
        acc[b // per_tile] += pltpu.roll(sums, (b % per_tile) * (BLK // LOOK_RG), 1)
        return 0

    lax.fori_loop(0, blocks // 2, combine, 0)

    def p_wait(s, _):
        slot = lax.rem(me + s, parties)
        p_copy(slot, slot, slot).wait_recv()
        return 0

    lax.fori_loop(1, parties, p_wait, 0)
    totals[pl.ds(me, 1)] = (jnp.sum(parts[...], axis=0) * (scale / parties))[None]

    def t_copy(slot, peer):
        return pltpu.make_async_remote_copy(
            src_ref=totals.at[slot], dst_ref=totals.at[slot], send_sem=t_s.at[peer], recv_sem=t_r.at[slot],
            device_id={"date": peer}, device_id_type=MESH)

    def t_send(s, _):
        t_copy(me, lax.rem(me + s, parties)).start()
        return 0

    lax.fori_loop(1, parties, t_send, 0)
    lax.fori_loop(blocks // 2, blocks, combine, 0)

    lane_tile = min(BLK, ifg_ref.shape[2])
    for t in range(ifg_ref.shape[2] // lane_tile):
        lanes = slice(t * lane_tile, (t + 1) * lane_tile)
        real, imag, ref = (acc[t, q * looks_out : (q + 1) * looks_out, :] * scale for q in range(3))
        normalizer = 1.0 / jnp.sqrt(ref * (acc_sec[t] * scale) + EPSILON)
        ifg_ref[0, :, lanes] = real * normalizer
        ifg_ref[1, :, lanes] = imag * normalizer

    def t_wait(s, _):
        slot = lax.rem(me + s, parties)
        t_copy(slot, slot).wait_recv()
        return 0

    lax.fori_loop(1, parties, t_wait, 0)
    for d in range(parties):
        stack_ref[2 * (d % per_slab) : 2 * (d % per_slab) + 2, (d // per_slab) * BLK : (d // per_slab + 1) * BLK] = totals[d]

    def sent(s, _):
        peer = lax.rem(me + s, parties)
        rc_copy(me, peer).wait_send()
        p_copy(peer, me, peer).wait_send()
        t_copy(me, peer).wait_send()
        return 0

    lax.fori_loop(1, parties, sent, 0)

    def z_sent(s, _):
        peer = z_index(s) + my_y * 2 + my_c
        m_copy(me, peer, 0, peer).wait_send()
        return 0

    def forward_sent(s, _):
        near = z_index(s) + my_y * 2 + my_c
        far = z_index(s) + (1 - my_y) * 2 + my_c
        m_copy(near, across, 1, near).wait_send()
        m_copy(near, twin, 2, near).wait_send()
        m_copy(far, twin, 2, far).wait_send()
        return 0

    lax.fori_loop(1, deep, z_sent, 0)
    lax.fori_loop(0, deep, forward_sent, 0)


def per_device(
    parties, x, master, rate, center, row_pos, row_frac, row_band, col_pos, col_frac, col_band,
):
    lines_in, cells = x.shape[2], x.shape[3]
    samples = col_pos.shape[1]
    rows_out = row_pos.shape[1]
    blocks = samples // BLK
    looks_out, look_lanes = rows_out // LOOK_AZ, samples // LOOK_RG
    tiles = -(-look_lanes // BLK)
    tiles_in = (cells - HALF) // BLK
    vmem = pl.BlockSpec(memory_space=pltpu.VMEM)
    dma = pltpu.SemaphoreType.DMA
    f32, bf16 = jnp.float32, jnp.bfloat16
    ifg, stack = pl.pallas_call(
        functools.partial(kernel, parties),
        out_shape=(
            jax.ShapeDtypeStruct((2, looks_out, look_lanes), f32),
            jax.ShapeDtypeStruct((looks_out, look_lanes), f32),
        ),
        in_specs=[pl.BlockSpec(memory_space=pl.ANY)] + [vmem] * 7 + [pl.BlockSpec(memory_space=pltpu.SMEM)],
        out_specs=(vmem, vmem),
        scratch_shapes=[
            pltpu.VMEM((2, lines_in, cells), bf16),
            pltpu.VMEM((2 * tiles_in, 2, lines_in, BLK), bf16),
            pltpu.VMEM((TAPS, samples), f32),
            pltpu.VMEM((8, BLK), f32),
            pltpu.VMEM((parties, 8, BLK), f32),
            pltpu.VMEM((parties, 2, rows_out, BLK), bf16),
            pltpu.VMEM((blocks, 2, rows_out, BLK), bf16),
            pltpu.VMEM((rows_out, BLK), f32),
            pltpu.VMEM((rows_out, BLK), f32),
            pltpu.VMEM((tiles, 3 * looks_out, BLK), f32),
            pltpu.VMEM((tiles, looks_out, BLK), f32),
            pltpu.VMEM((parties, 2, BLK), f32),
            pltpu.VMEM((parties, 2, BLK), f32),
            pltpu.VMEM((parties, 2, BLK), f32),
            dma((tiles_in + 1,)),
            dma((parties,)), dma((parties,)),
            dma((3, parties)), dma((parties,)),
            dma((parties,)), dma((parties,)),
            dma((parties,)), dma((parties,)),
        ],
        compiler_params=pltpu.CompilerParams(
            collective_id=0, has_side_effects=True, vmem_limit_bytes=48 * 1024 * 1024
        ),
        cost_estimate=pl.CostEstimate(flops=6 * 10**8, bytes_accessed=4 * 10**6, transcendentals=0),
        name="coregister",
    )(x, master, rate[None], center[None], row_pos, row_frac, col_pos, col_frac, col_band)
    return ifg[None], stack


def solution(mesh):
    placed = (
        P(("parts", "date"), None, None, None),
        P(None, "parts", "date"),
        P("date"),
        P("date"),
        P(("parts", "date"), None),
        P(("parts", "date"), None),
        P(("parts", "date"), None),
        P(("parts", "date"), None),
        P(("parts", "date"), None),
        P(("parts", "date"), None),
    )
    return jax.shard_map(
        functools.partial(per_device, mesh.shape["date"]),
        mesh=mesh,
        in_specs=placed,
        out_specs=(P(("parts", "date"), None, None, None), P("parts", None)),
        check_vma=False,
    )
```

```python
import functools
import math

import jax
import jax.numpy as jnp
from jax import lax
from jax.experimental import pallas as pl
from jax.experimental.pallas import tpu as pltpu
from jax.sharding import PartitionSpec as P

TAPS = 8
LEAD = TAPS // 2 - 1
BLK = 128
WIN = 192
LOOK_AZ = 4
LOOK_RG = 16
HALF = 64
EPSILON = 1e-06
MESH = pl.DeviceIdType.MESH
SIN_TERMS = (4.442882919124343, -7.308245686509025, 3.6063542184321515, -0.8461116503693629, 0.10982451641673696)
COS_TERMS = (1.414213496255228, -6.978850948563791, 5.739460376906791, -1.8835579059844396, 0.3106880275224321)


def poly(terms, x):
    total = jnp.full_like(x, terms[-1])
    for term in terms[-2::-1]:
        total = total * x + term
    return total


def sincos_turns(turns):
    rest = turns - jnp.round(turns)
    square = rest * rest
    sine = rest * poly(SIN_TERMS, square)
    cosine = poly(COS_TERMS, square)
    return sine * cosine, 1.0 - sine * sine


def tap_weights(fraction):
    step = lax.broadcasted_iota(jnp.int32, (TAPS, fraction.shape[1]), 0) - LEAD
    spacing = step.astype(jnp.float32) - fraction
    angle = math.pi * spacing
    sine, _ = sincos_turns(spacing * 0.5)
    sinc = jnp.where(spacing == 0.0, 1.0, sine / jnp.where(spacing == 0.0, 1.0, angle))
    _, cosine = sincos_turns(spacing * 0.125)
    return sinc * (0.5 + 0.5 * cosine)


def tap_matrix(first, weights, cells):
    cell = lax.broadcasted_iota(jnp.int32, (cells, first.shape[1]), 0) - first
    total = jnp.zeros(cell.shape, jnp.float32)
    for k in range(TAPS):
        total = jnp.where(cell == k, weights[k : k + 1], total)
    return total.astype(jnp.bfloat16)


def slab_sum(values):
    rows = values.shape[0] // LOOK_AZ
    total = values[:rows]
    for b in range(1, LOOK_AZ):
        total = total + values[b * rows : (b + 1) * rows]
    return total


def looked(values, gather):
    high = values.astype(jnp.bfloat16)
    low = (values - high.astype(jnp.float32)).astype(jnp.bfloat16)
    return jnp.dot(jnp.concatenate([high, low], axis=1), gather, preferred_element_type=jnp.float32)


def kernel(
    parties,
    x_hbm, master_hbm, rate_hbm, center_hbm, row_pos_hbm, row_frac_hbm, col_pos_hbm, col_frac_hbm, col_band_hbm,
    ifg_ref, stack_ref,
    master_ref, rate_ref, center_ref, row_pos, row_frac, col_pos, col_frac, col_band,
    x0, xs, weights, own_rc, rc, mg, res, times, place, acc, acc_sec, chunks, parts, totals,
    small_sems, in_sems, rc_s, rc_r, m_s, m_r, p_s, p_r, t_s, t_r,
):
    me = lax.axis_index("date")
    lines_in = x0.shape[1]
    tiles_in = xs.shape[0] // 2
    last_half = xs.shape[0] - 3
    blocks = col_pos.shape[1] // BLK
    rows_out = row_pos.shape[1]
    looks_out = rows_out // LOOK_AZ
    per_tile = BLK * LOOK_RG // BLK

    small = [
        pltpu.make_async_copy(source, target, small_sems.at[i])
        for i, (source, target) in enumerate((
            (master_hbm, master_ref), (rate_hbm, rate_ref), (center_hbm, center_ref), (col_frac_hbm, col_frac),
            (row_pos_hbm, row_pos), (row_frac_hbm, row_frac), (col_pos_hbm, col_pos), (col_band_hbm, col_band)))
    ]
    for copy in small:
        copy.start()
    fetch0 = pltpu.make_async_copy(x_hbm.at[0], x0, in_sems.at[0])
    fetch0.start()

    def tile_copy(t):
        lanes = pl.ds(pl.multiple_of(t * BLK, BLK), BLK)
        return pltpu.make_async_copy(x_hbm.at[0, :, :, lanes], xs.at[2 * t], in_sems.at[t + 1])

    def tile_start(t, _):
        tile_copy(t).start()
        return 0

    def tile_wait(t, _):
        tile_copy(t).wait()
        return 0

    lax.fori_loop(0, tiles_in, tile_start, 0)

    barrier = pltpu.get_barrier_semaphore()

    def greet(s, _):
        pl.semaphore_signal(barrier, inc=1, device_id={"date": lax.rem(me + s, parties)}, device_id_type=MESH)
        return 0

    lax.fori_loop(1, parties, greet, 0)

    for copy in small[:3]:
        copy.wait()

    own_rc[...] = jnp.zeros_like(own_rc)
    own_rc[0:1, :] = rate_ref[...] * (0.5 / math.pi)
    own_rc[1:2, :] = center_ref[...]
    rc[pl.ds(me, 1)] = own_rc[...][None]
    to = lax.broadcasted_iota(jnp.int32, (rows_out, rows_out), 0)
    source = lax.broadcasted_iota(jnp.int32, (rows_out, rows_out), 1)
    order = jnp.where(source == LOOK_AZ * (to % looks_out) + to // looks_out, 1.0, 0.0).astype(jnp.bfloat16)
    for p in range(2):
        mg[pl.ds(me, 1), p] = jnp.dot(order, master_ref[p], preferred_element_type=jnp.float32).astype(jnp.bfloat16)[None]

    pl.semaphore_wait(barrier, parties - 1)

    def rc_copy(slot, peer):
        return pltpu.make_async_remote_copy(
            src_ref=own_rc, dst_ref=rc.at[slot], send_sem=rc_s.at[peer], recv_sem=rc_r.at[slot],
            device_id={"date": peer}, device_id_type=MESH)

    def rc_send(s, _):
        rc_copy(me, lax.rem(me + s, parties)).start()
        return 0

    lax.fori_loop(1, parties, rc_send, 0)

    deep = parties // 4
    my_z, my_y, my_c = me // 4, (me // 2) % 2, me % 2
    across = my_z * 4 + (1 - my_y) * 2 + my_c
    twin = my_z * 4 + my_y * 2 + (1 - my_c)

    def m_copy(slot, peer, kind, tag):
        return pltpu.make_async_remote_copy(
            src_ref=mg.at[slot], dst_ref=mg.at[slot], send_sem=m_s.at[kind, tag], recv_sem=m_r.at[slot],
            device_id={"date": peer}, device_id_type=MESH)

    def z_index(s):
        return lax.rem(my_z + s, deep) * 4

    def z_send(s, _):
        peer = z_index(s) + my_y * 2 + my_c
        m_copy(me, peer, 0, peer).start()
        return 0

    m_copy(me, across, 1, me).start()
    lax.fori_loop(1, deep, z_send, 0)
    m_copy(me, twin, 2, me).start()

    def z_pass(s, _):
        slot = z_index(s) + my_y * 2 + my_c
        m_copy(slot, slot, 0, slot).wait_recv()
        m_copy(slot, across, 1, slot).start()
        m_copy(slot, twin, 2, slot).start()
        return 0

    def y_pass(s, _):
        slot = z_index(s) + (1 - my_y) * 2 + my_c
        m_copy(slot, across, 1, slot).wait_recv()
        m_copy(slot, twin, 2, slot).start()
        return 0

    def twin_wait(s, _):
        for y in range(2):
            slot = z_index(s) + y * 2 + (1 - my_c)
            m_copy(slot, twin, 2, slot).wait_recv()
        return 0

    for copy in small[3:]:
        copy.wait()

    weights[...] = tap_weights(col_frac[...])
    row_taps = tap_matrix(row_pos[...] - LEAD, tap_weights(row_frac[...]), lines_in)
    row_taps = lax.dot_general(
        order, row_taps, (((1,), (1,)), ((), ())), preferred_element_type=jnp.float32
    ).astype(jnp.bfloat16)
    when = (row_pos[...].astype(jnp.float32) + row_frac[...]) / lines_in
    times[...] = jnp.transpose(jnp.broadcast_to(when, (BLK, rows_out)))
    for b in range(LOOK_AZ):
        place[b * looks_out : (b + 1) * looks_out, :] = times[pl.ds(b, looks_out, stride=LOOK_AZ), :]
    lane = lax.broadcasted_iota(jnp.int32, (2 * BLK, BLK), 0) % BLK
    out_lane = lax.broadcasted_iota(jnp.int32, (2 * BLK, BLK), 1)
    gather = jnp.where(lane // LOOK_RG == out_lane, 1.0, 0.0).astype(jnp.bfloat16)
    acc[...] = jnp.zeros_like(acc)
    acc_sec[...] = jnp.zeros_like(acc_sec)

    fetch0.wait()
    lax.fori_loop(0, tiles_in, tile_wait, 0)
    for t in range(tiles_in):
        xs[2 * t + 1] = x0[:, :, t * BLK + HALF : (t + 1) * BLK + HALF]

    def rc_wait(s, _):
        slot = lax.rem(me + s, parties)
        rc_copy(slot, slot).wait_recv()
        return 0

    lax.fori_loop(1, parties, rc_wait, 0)

    line_time = lax.broadcasted_iota(jnp.int32, (lines_in, BLK), 0).astype(jnp.float32) / lines_in

    def resample(b, _):
        half = lax.min(lax.div(col_band[0, b], HALF), last_half)
        window = jnp.concatenate([xs[half], xs[half + 2]], axis=2).reshape(2 * lines_in, 2 * BLK)
        columns = pl.ds(pl.multiple_of(b * BLK, BLK), BLK)
        taps = tap_matrix(col_pos[:, columns] - (LEAD + HALF * half), weights[:, columns], 2 * BLK)
        ranged = jnp.dot(window, taps, preferred_element_type=jnp.float32)
        rate, center = rc[b, 0:1, :], rc[b, 1:2, :]
        offset = line_time - center
        sine, cosine = sincos_turns(rate * offset * offset)
        real, imag = ranged[:lines_in], ranged[lines_in:]
        deramped = jnp.concatenate(
            [(real * cosine + imag * sine).astype(jnp.bfloat16), (imag * cosine - real * sine).astype(jnp.bfloat16)],
            axis=1)
        moved = jnp.dot(row_taps, deramped, preferred_element_type=jnp.float32)
        offset = place[...] - center
        sine, cosine = sincos_turns(rate * offset * offset)
        real, imag = moved[:, :BLK], moved[:, BLK:]
        real, imag = (
            (real * cosine - imag * sine).astype(jnp.bfloat16),
            (real * sine + imag * cosine).astype(jnp.bfloat16),
        )
        res[b, 0] = real
        res[b, 1] = imag
        real, imag = real.astype(jnp.float32), imag.astype(jnp.float32)
        sums = looked(slab_sum(real * real + imag * imag), gather)
        acc_sec[b // per_tile] += pltpu.roll(sums, (b % per_tile) * (BLK // LOOK_RG), 1)
        return 0

    cut = blocks // 2
    lax.fori_loop(0, cut, resample, 0)
    lax.fori_loop(1, deep, z_pass, 0)
    lax.fori_loop(cut, blocks, resample, 0)
    lax.fori_loop(0, deep, y_pass, 0)

    per_slab = looks_out // 2
    scale = 1.0 / (LOOK_AZ * LOOK_RG)
    for d in range(parties):
        chunks[d] = acc_sec[d // per_slab, 2 * (d % per_slab) : 2 * (d % per_slab) + 2, :]

    def p_copy(chunk, slot, peer):
        return pltpu.make_async_remote_copy(
            src_ref=chunks.at[chunk], dst_ref=parts.at[slot], send_sem=p_s.at[peer], recv_sem=p_r.at[slot],
            device_id={"date": peer}, device_id_type=MESH)

    def p_send(s, _):
        peer = lax.rem(me + s, parties)
        p_copy(peer, me, peer).start()
        return 0

    lax.fori_loop(1, parties, p_send, 0)
    parts[pl.ds(me, 1)] = chunks[pl.ds(me, 1)]

    lax.fori_loop(0, deep, twin_wait, 0)

    def combine(b, _):
        m0, m1 = mg[b, 0].astype(jnp.float32), mg[b, 1].astype(jnp.float32)
        r0, r1 = res[b, 0].astype(jnp.float32), res[b, 1].astype(jnp.float32)
        rows = jnp.concatenate(
            [slab_sum(m0 * r0 + m1 * r1), slab_sum(m1 * r0 - m0 * r1), slab_sum(m0 * m0 + m1 * m1)], axis=0)
        sums = looked(rows, gather)
        acc[b // per_tile] += pltpu.roll(sums, (b % per_tile) * (BLK // LOOK_RG), 1)
        return 0

    lax.fori_loop(0, blocks // 2, combine, 0)

    def p_wait(s, _):
        slot = lax.rem(me + s, parties)
        p_copy(slot, slot, slot).wait_recv()
        return 0

    lax.fori_loop(1, parties, p_wait, 0)
    totals[pl.ds(me, 1)] = (jnp.sum(parts[...], axis=0) * (scale / parties))[None]

    def t_copy(slot, peer):
        return pltpu.make_async_remote_copy(
            src_ref=totals.at[slot], dst_ref=totals.at[slot], send_sem=t_s.at[peer], recv_sem=t_r.at[slot],
            device_id={"date": peer}, device_id_type=MESH)

    def t_send(s, _):
        t_copy(me, lax.rem(me + s, parties)).start()
        return 0

    lax.fori_loop(1, parties, t_send, 0)
    lax.fori_loop(blocks // 2, blocks, combine, 0)

    lane_tile = min(BLK, ifg_ref.shape[2])
    for t in range(ifg_ref.shape[2] // lane_tile):
        lanes = slice(t * lane_tile, (t + 1) * lane_tile)
        real, imag, ref = (acc[t, q * looks_out : (q + 1) * looks_out, :] * scale for q in range(3))
        normalizer = 1.0 / jnp.sqrt(ref * (acc_sec[t] * scale) + EPSILON)
        ifg_ref[0, :, lanes] = real * normalizer
        ifg_ref[1, :, lanes] = imag * normalizer

    def t_wait(s, _):
        slot = lax.rem(me + s, parties)
        t_copy(slot, slot).wait_recv()
        return 0

    lax.fori_loop(1, parties, t_wait, 0)
    for d in range(parties):
        stack_ref[2 * (d % per_slab) : 2 * (d % per_slab) + 2, (d // per_slab) * BLK : (d // per_slab + 1) * BLK] = totals[d]

    def sent(s, _):
        peer = lax.rem(me + s, parties)
        rc_copy(me, peer).wait_send()
        p_copy(peer, me, peer).wait_send()
        t_copy(me, peer).wait_send()
        return 0

    lax.fori_loop(1, parties, sent, 0)

    def z_sent(s, _):
        peer = z_index(s) + my_y * 2 + my_c
        m_copy(me, peer, 0, peer).wait_send()
        return 0

    def forward_sent(s, _):
        near = z_index(s) + my_y * 2 + my_c
        far = z_index(s) + (1 - my_y) * 2 + my_c
        m_copy(near, across, 1, near).wait_send()
        m_copy(near, twin, 2, near).wait_send()
        m_copy(far, twin, 2, far).wait_send()
        return 0

    lax.fori_loop(1, deep, z_sent, 0)
    lax.fori_loop(0, deep, forward_sent, 0)


def per_device(
    parties, x, master, rate, center, row_pos, row_frac, row_band, col_pos, col_frac, col_band,
):
    lines_in, cells = x.shape[2], x.shape[3]
    samples = col_pos.shape[1]
    rows_out = row_pos.shape[1]
    blocks = samples // BLK
    looks_out, look_lanes = rows_out // LOOK_AZ, samples // LOOK_RG
    tiles = -(-look_lanes // BLK)
    tiles_in = (cells - HALF) // BLK
    vmem = pl.BlockSpec(memory_space=pltpu.VMEM)
    dma = pltpu.SemaphoreType.DMA
    f32, bf16 = jnp.float32, jnp.bfloat16
    ifg, stack = pl.pallas_call(
        functools.partial(kernel, parties),
        out_shape=(
            jax.ShapeDtypeStruct((2, looks_out, look_lanes), f32),
            jax.ShapeDtypeStruct((looks_out, look_lanes), f32),
        ),
        in_specs=[pl.BlockSpec(memory_space=pl.ANY)] * 9,
        out_specs=(vmem, vmem),
        scratch_shapes=[
            pltpu.VMEM(master.shape, bf16),
            pltpu.VMEM((1, BLK), f32),
            pltpu.VMEM((1, BLK), f32),
            pltpu.VMEM(row_pos.shape, jnp.int32),
            pltpu.VMEM(row_frac.shape, f32),
            pltpu.VMEM(col_pos.shape, jnp.int32),
            pltpu.VMEM(col_frac.shape, f32),
            pltpu.SMEM(col_band.shape, jnp.int32),
            pltpu.VMEM((2, lines_in, cells), bf16),
            pltpu.VMEM((2 * tiles_in, 2, lines_in, BLK), bf16),
            pltpu.VMEM((TAPS, samples), f32),
            pltpu.VMEM((8, BLK), f32),
            pltpu.VMEM((parties, 8, BLK), f32),
            pltpu.VMEM((parties, 2, rows_out, BLK), bf16),
            pltpu.VMEM((blocks, 2, rows_out, BLK), bf16),
            pltpu.VMEM((rows_out, BLK), f32),
            pltpu.VMEM((rows_out, BLK), f32),
            pltpu.VMEM((tiles, 3 * looks_out, BLK), f32),
            pltpu.VMEM((tiles, looks_out, BLK), f32),
            pltpu.VMEM((parties, 2, BLK), f32),
            pltpu.VMEM((parties, 2, BLK), f32),
            pltpu.VMEM((parties, 2, BLK), f32),
            dma((8,)),
            dma((tiles_in + 1,)),
            dma((parties,)), dma((parties,)),
            dma((3, parties)), dma((parties,)),
            dma((parties,)), dma((parties,)),
            dma((parties,)), dma((parties,)),
        ],
        compiler_params=pltpu.CompilerParams(
            collective_id=0, has_side_effects=True, vmem_limit_bytes=60 * 1024 * 1024
        ),
        cost_estimate=pl.CostEstimate(flops=6 * 10**8, bytes_accessed=4 * 10**6, transcendentals=0),
        name="coregister",
    )(x, master, rate[None], center[None], row_pos, row_frac, col_pos, col_frac, col_band)
    return ifg[None], stack


def solution(mesh):
    placed = (
        P(("parts", "date"), None, None, None),
        P(None, "parts", "date"),
        P("date"),
        P("date"),
        P(("parts", "date"), None),
        P(("parts", "date"), None),
        P(("parts", "date"), None),
        P(("parts", "date"), None),
        P(("parts", "date"), None),
        P(("parts", "date"), None),
    )
    return jax.shard_map(
        functools.partial(per_device, mesh.shape["date"]),
        mesh=mesh,
        in_specs=placed,
        out_specs=(P(("parts", "date"), None, None, None), P("parts", None)),
        check_vma=False,
    )
```

```python
import functools
import math

import jax
import jax.numpy as jnp
from jax import lax
from jax.experimental import pallas as pl
from jax.experimental.pallas import tpu as pltpu
from jax.sharding import PartitionSpec as P

TAPS = 8
LEAD = TAPS // 2 - 1
BLK = 128
WIN = 192
LOOK_AZ = 4
LOOK_RG = 16
HALF = 64
EPSILON = 1e-06
MESH = pl.DeviceIdType.MESH
SIN_TERMS = (4.442882919124343, -7.308245686509025, 3.6063542184321515, -0.8461116503693629, 0.10982451641673696)
COS_TERMS = (1.414213496255228, -6.978850948563791, 5.739460376906791, -1.8835579059844396, 0.3106880275224321)


def poly(terms, x):
    total = jnp.full_like(x, terms[-1])
    for term in terms[-2::-1]:
        total = total * x + term
    return total


def sincos_turns(turns):
    rest = turns - jnp.round(turns)
    square = rest * rest
    sine = rest * poly(SIN_TERMS, square)
    cosine = poly(COS_TERMS, square)
    return sine * cosine, 1.0 - sine * sine


def tap_weights(fraction):
    step = lax.broadcasted_iota(jnp.int32, (TAPS, fraction.shape[1]), 0) - LEAD
    spacing = step.astype(jnp.float32) - fraction
    angle = math.pi * spacing
    sine, _ = sincos_turns(spacing * 0.5)
    sinc = jnp.where(spacing == 0.0, 1.0, sine / jnp.where(spacing == 0.0, 1.0, angle))
    _, cosine = sincos_turns(spacing * 0.125)
    return sinc * (0.5 + 0.5 * cosine)


def tap_matrix(first, weights, cells):
    cell = lax.broadcasted_iota(jnp.int32, (cells, first.shape[1]), 0) - first
    total = jnp.zeros(cell.shape, jnp.float32)
    for k in range(TAPS):
        total = jnp.where(cell == k, weights[k : k + 1], total)
    return total.astype(jnp.bfloat16)


def slab_sum(values):
    rows = values.shape[0] // LOOK_AZ
    total = values[:rows]
    for b in range(1, LOOK_AZ):
        total = total + values[b * rows : (b + 1) * rows]
    return total


def looked(values, gather):
    high = values.astype(jnp.bfloat16)
    low = (values - high.astype(jnp.float32)).astype(jnp.bfloat16)
    return jnp.dot(jnp.concatenate([high, low], axis=1), gather, preferred_element_type=jnp.float32)


def kernel(
    parties,
    x_hbm, master_hbm, rate_hbm, center_hbm, row_pos_hbm, row_frac_hbm, col_pos_hbm, col_frac_hbm, col_band_hbm,
    out_ref,
    master_ref, rate_ref, center_ref, row_pos, row_frac, col_pos, col_frac, col_band,
    x0, xs, weights, own_rc, rc, mg, res, times, place, acc, sec, outgoing, powers,
    small_sems, in_sems, rc_s, rc_r, m_s, m_r, p_s, p_r,
):
    me = lax.axis_index("date")
    deep = parties // 4
    my_z, my_y, my_c = me // 4, (me // 2) % 2, me % 2
    across = my_z * 4 + (1 - my_y) * 2 + my_c
    twin = my_z * 4 + my_y * 2 + (1 - my_c)
    lines_in = x0.shape[1]
    tiles_in = xs.shape[0] // 2
    last_half = xs.shape[0] - 3
    blocks = col_pos.shape[1] // BLK
    rows_out = row_pos.shape[1]
    looks_out = rows_out // LOOK_AZ
    shift = BLK // LOOK_RG
    per_tile = BLK // shift
    per_part = per_tile // 2
    part_steps = per_part // 2

    small = [
        pltpu.make_async_copy(source, target, small_sems.at[i])
        for i, (source, target) in enumerate((
            (master_hbm, master_ref), (rate_hbm, rate_ref), (center_hbm, center_ref), (col_frac_hbm, col_frac),
            (row_pos_hbm, row_pos), (row_frac_hbm, row_frac), (col_pos_hbm, col_pos), (col_band_hbm, col_band)))
    ]
    for copy in small:
        copy.start()
    fetch0 = pltpu.make_async_copy(x_hbm.at[0], x0, in_sems.at[0])
    fetch0.start()

    def tile_copy(t):
        lanes = pl.ds(pl.multiple_of(t * BLK, BLK), BLK)
        return pltpu.make_async_copy(x_hbm.at[0, :, :, lanes], xs.at[2 * t], in_sems.at[t + 1])

    def tile_start(t, _):
        tile_copy(t).start()
        return 0

    def tile_wait(t, _):
        tile_copy(t).wait()
        return 0

    lax.fori_loop(0, tiles_in, tile_start, 0)

    barrier = pltpu.get_barrier_semaphore()

    def greet(s, _):
        pl.semaphore_signal(barrier, inc=1, device_id={"date": lax.rem(me + s, parties)}, device_id_type=MESH)
        return 0

    lax.fori_loop(1, parties, greet, 0)

    for copy in small[:3]:
        copy.wait()

    own_rc[...] = jnp.zeros_like(own_rc)
    own_rc[0:1, :] = rate_ref[...] * (0.5 / math.pi)
    own_rc[1:2, :] = center_ref[...]
    rc[pl.ds(me, 1)] = own_rc[...][None]
    to = lax.broadcasted_iota(jnp.int32, (rows_out, rows_out), 0)
    source = lax.broadcasted_iota(jnp.int32, (rows_out, rows_out), 1)
    order = jnp.where(source == LOOK_AZ * (to % looks_out) + to // looks_out, 1.0, 0.0).astype(jnp.bfloat16)
    for p in range(2):
        mg[pl.ds(me, 1), p] = jnp.dot(order, master_ref[p], preferred_element_type=jnp.float32).astype(jnp.bfloat16)[None]

    pl.semaphore_wait(barrier, parties - 1)

    def rc_copy(slot, peer):
        return pltpu.make_async_remote_copy(
            src_ref=own_rc, dst_ref=rc.at[slot], send_sem=rc_s, recv_sem=rc_r,
            device_id={"date": peer}, device_id_type=MESH)

    def rc_all():
        every = rc.at[pl.ds(0, parties - 1)]
        return pltpu.make_async_remote_copy(
            src_ref=every, dst_ref=every, send_sem=rc_s, recv_sem=rc_r,
            device_id={"date": twin}, device_id_type=MESH)

    def rc_send(s, _):
        rc_copy(me, lax.rem(me + s, parties)).start()
        return 0

    lax.fori_loop(1, parties, rc_send, 0)


    def m_copy(slot, peer, kind, tag):
        return pltpu.make_async_remote_copy(
            src_ref=mg.at[slot], dst_ref=mg.at[slot], send_sem=m_s.at[kind, tag], recv_sem=m_r.at[slot],
            device_id={"date": peer}, device_id_type=MESH)

    def z_index(s):
        return lax.rem(my_z + s, deep) * 4

    def z_send(s, _):
        peer = z_index(s) + my_y * 2 + my_c
        m_copy(me, peer, 0, peer).start()
        return 0

    m_copy(me, across, 1, me).start()
    lax.fori_loop(1, deep, z_send, 0)
    m_copy(me, twin, 2, me).start()

    def z_pass(s, _):
        slot = z_index(s) + my_y * 2 + my_c
        m_copy(slot, slot, 0, slot).wait_recv()
        m_copy(slot, across, 1, slot).start()
        m_copy(slot, twin, 2, slot).start()
        return 0

    def y_pass(s, _):
        slot = z_index(s) + (1 - my_y) * 2 + my_c
        m_copy(slot, across, 1, slot).wait_recv()
        m_copy(slot, twin, 2, slot).start()
        return 0

    def twin_wait(s, _):
        for y in range(2):
            slot = z_index(s) + y * 2 + (1 - my_c)
            m_copy(slot, twin, 2, slot).wait_recv()
        return 0

    for copy in small[3:]:
        copy.wait()

    weights[...] = tap_weights(col_frac[...])
    row_taps = tap_matrix(row_pos[...] - LEAD, tap_weights(row_frac[...]), lines_in)
    row_taps = lax.dot_general(
        order, row_taps, (((1,), (1,)), ((), ())), preferred_element_type=jnp.float32
    ).astype(jnp.bfloat16)
    when = (row_pos[...].astype(jnp.float32) + row_frac[...]) / lines_in
    times[...] = jnp.transpose(jnp.broadcast_to(when, (BLK, rows_out)))
    for b in range(LOOK_AZ):
        place[b * looks_out : (b + 1) * looks_out, :] = times[pl.ds(b, looks_out, stride=LOOK_AZ), :]
    lane = lax.broadcasted_iota(jnp.int32, (2 * BLK, BLK), 0) % BLK
    out_lane = lax.broadcasted_iota(jnp.int32, (2 * BLK, BLK), 1)
    gather = jnp.where(lane // LOOK_RG == out_lane, 1.0, 0.0).astype(jnp.bfloat16)
    acc[...] = jnp.zeros_like(acc)
    sec[...] = jnp.zeros_like(sec)

    fetch0.wait()
    lax.fori_loop(0, tiles_in, tile_wait, 0)
    for t in range(tiles_in):
        xs[2 * t + 1] = x0[:, :, t * BLK + HALF : (t + 1) * BLK + HALF]

    rc_all().wait_recv()

    line_time = lax.broadcasted_iota(jnp.int32, (lines_in, BLK), 0).astype(jnp.float32) / lines_in

    def resample(b):
        half = lax.min(lax.div(col_band[0, b], HALF), last_half)
        window = jnp.concatenate([xs[half], xs[half + 2]], axis=2).reshape(2 * lines_in, 2 * BLK)
        columns = pl.ds(pl.multiple_of(b * BLK, BLK), BLK)
        taps = tap_matrix(col_pos[:, columns] - (LEAD + HALF * half), weights[:, columns], 2 * BLK)
        ranged = jnp.dot(window, taps, preferred_element_type=jnp.float32)
        rate, center = rc[b, 0:1, :], rc[b, 1:2, :]
        offset = line_time - center
        sine, cosine = sincos_turns(rate * offset * offset)
        real, imag = ranged[:lines_in], ranged[lines_in:]
        deramped = jnp.concatenate(
            [(real * cosine + imag * sine).astype(jnp.bfloat16), (imag * cosine - real * sine).astype(jnp.bfloat16)],
            axis=1)
        moved = jnp.dot(row_taps, deramped, preferred_element_type=jnp.float32)
        offset = place[...] - center
        sine, cosine = sincos_turns(rate * offset * offset)
        real, imag = moved[:, :BLK], moved[:, BLK:]
        real, imag = (
            (real * cosine - imag * sine).astype(jnp.bfloat16),
            (real * sine + imag * cosine).astype(jnp.bfloat16),
        )
        res[b, 0] = real
        res[b, 1] = imag
        real, imag = real.astype(jnp.float32), imag.astype(jnp.float32)
        sums = looked(slab_sum(real * real + imag * imag), gather)
        sec[b // per_part] += pltpu.roll(sums, (b % per_part) * shift, 1)

    def p_copy(part, peer):
        return pltpu.make_async_remote_copy(
            src_ref=outgoing.at[part], dst_ref=powers.at[part, me], send_sem=p_s.at[part], recv_sem=p_r.at[part],
            device_id={"date": peer}, device_id_type=MESH)

    def p_all(part):
        every = powers.at[part, pl.ds(0, parties - 1)]
        return pltpu.make_async_remote_copy(
            src_ref=every, dst_ref=every, send_sem=p_s.at[part], recv_sem=p_r.at[part],
            device_id={"date": twin}, device_id_type=MESH)

    def step(i, _):
        resample(2 * i)
        resample(2 * i + 1)

        @pl.when(i == 1)
        def _():
            lax.fori_loop(1, deep, z_pass, 0)

        @pl.when(i == 5)
        def _():
            lax.fori_loop(0, deep, y_pass, 0)

        @pl.when(i % part_steps == part_steps - 1)
        def _():
            part = i // part_steps
            here = sec[part]
            packed = here[: looks_out // 2] + pltpu.roll(here[looks_out // 2 :], BLK // 2, 1)
            packed = packed.astype(jnp.bfloat16)
            outgoing[part] = packed
            powers[part, pl.ds(me, 1)] = packed[None]

            def p_send(s, _):
                p_copy(part, lax.rem(me + s, parties)).start()
                return 0

            lax.fori_loop(1, parties, p_send, 0)

        return 0

    lax.fori_loop(0, blocks // 2, step, 0)
    lax.fori_loop(0, deep, twin_wait, 0)

    def combine(b):
        m0, m1 = mg[b, 0].astype(jnp.float32), mg[b, 1].astype(jnp.float32)
        r0, r1 = res[b, 0].astype(jnp.float32), res[b, 1].astype(jnp.float32)
        rows = jnp.concatenate(
            [slab_sum(m0 * r0 + m1 * r1), slab_sum(m1 * r0 - m0 * r1), slab_sum(m0 * m0 + m1 * m1)], axis=0)
        sums = looked(rows, gather)
        acc[b // per_tile] += pltpu.roll(sums, (b % per_tile) * shift, 1)

    def combine_step(i, _):
        combine(2 * i)
        combine(2 * i + 1)
        return 0

    lax.fori_loop(0, blocks // 2, combine_step, 0)

    scale = 1.0 / (LOOK_AZ * LOOK_RG)
    left = lax.broadcasted_iota(jnp.int32, (looks_out // 2, BLK), 1) < BLK // 2
    for t in range(blocks // per_tile):
        lanes = slice(t * BLK, (t + 1) * BLK)
        real, imag, ref = (acc[t, q * looks_out : (q + 1) * looks_out, :] * scale for q in range(3))
        mine = (sec[2 * t] + pltpu.roll(sec[2 * t + 1], BLK // 2, 1)) * scale
        normalizer = 1.0 / jnp.sqrt(ref * mine + EPSILON)
        out_ref[0, :, lanes] = real * normalizer
        out_ref[1, :, lanes] = imag * normalizer
    for t in range(blocks // per_tile):
        lanes = slice(t * BLK, (t + 1) * BLK)
        p_all(2 * t).wait_recv()
        p_all(2 * t + 1).wait_recv()
        first, second = (
            jnp.sum(powers[2 * t + q].astype(jnp.float32), axis=0) * (scale / parties) for q in range(2))
        out_ref[2, : looks_out // 2, lanes] = jnp.where(left, first, pltpu.roll(second, BLK // 2, 1))
        out_ref[2, looks_out // 2 :, lanes] = jnp.where(left, pltpu.roll(first, BLK // 2, 1), second)

    rc_all().wait_send()
    for part in range(blocks // per_part):
        p_all(part).wait_send()

    def z_sent(s, _):
        peer = z_index(s) + my_y * 2 + my_c
        m_copy(me, peer, 0, peer).wait_send()
        return 0

    def forward_sent(s, _):
        near = z_index(s) + my_y * 2 + my_c
        far = z_index(s) + (1 - my_y) * 2 + my_c
        m_copy(near, across, 1, near).wait_send()
        m_copy(near, twin, 2, near).wait_send()
        m_copy(far, twin, 2, far).wait_send()
        return 0

    lax.fori_loop(1, deep, z_sent, 0)
    lax.fori_loop(0, deep, forward_sent, 0)


def per_device(
    parties, x, master, rate, center, row_pos, row_frac, row_band, col_pos, col_frac, col_band,
):
    lines_in, cells = x.shape[2], x.shape[3]
    samples = col_pos.shape[1]
    rows_out = row_pos.shape[1]
    blocks = samples // BLK
    looks_out, look_lanes = rows_out // LOOK_AZ, samples // LOOK_RG
    tiles = -(-look_lanes // BLK)
    tiles_in = (cells - HALF) // BLK
    vmem = pl.BlockSpec(memory_space=pltpu.VMEM)
    dma = pltpu.SemaphoreType.DMA
    f32, bf16 = jnp.float32, jnp.bfloat16
    out = pl.pallas_call(
        functools.partial(kernel, parties),
        out_shape=jax.ShapeDtypeStruct((3, looks_out, look_lanes), f32),
        in_specs=[pl.BlockSpec(memory_space=pl.ANY)] * 9,
        out_specs=vmem,
        scratch_shapes=[
            pltpu.VMEM(master.shape, bf16),
            pltpu.VMEM((1, BLK), f32),
            pltpu.VMEM((1, BLK), f32),
            pltpu.VMEM(row_pos.shape, jnp.int32),
            pltpu.VMEM(row_frac.shape, f32),
            pltpu.VMEM(col_pos.shape, jnp.int32),
            pltpu.VMEM(col_frac.shape, f32),
            pltpu.SMEM(col_band.shape, jnp.int32),
            pltpu.VMEM((2, lines_in, cells), bf16),
            pltpu.VMEM((2 * tiles_in, 2, lines_in, BLK), bf16),
            pltpu.VMEM((TAPS, samples), f32),
            pltpu.VMEM((8, BLK), f32),
            pltpu.VMEM((parties, 8, BLK), f32),
            pltpu.VMEM((parties, 2, rows_out, BLK), bf16),
            pltpu.VMEM((blocks, 2, rows_out, BLK), bf16),
            pltpu.VMEM((rows_out, BLK), f32),
            pltpu.VMEM((rows_out, BLK), f32),
            pltpu.VMEM((tiles, 3 * looks_out, BLK), f32),
            pltpu.VMEM((2 * tiles, looks_out, BLK), f32),
            pltpu.VMEM((2 * tiles, looks_out // 2, BLK), bf16),
            pltpu.VMEM((2 * tiles, parties, looks_out // 2, BLK), bf16),
            dma((8,)),
            dma((tiles_in + 1,)),
            dma, dma,
            dma((3, parties)), dma((parties,)),
            dma((2 * tiles,)), dma((2 * tiles,)),
        ],
        compiler_params=pltpu.CompilerParams(
            collective_id=0, has_side_effects=True, vmem_limit_bytes=60 * 1024 * 1024
        ),
        cost_estimate=pl.CostEstimate(flops=6 * 10**8, bytes_accessed=4 * 10**6, transcendentals=0),
        name="coregister",
    )(x, master, rate[None], center[None], row_pos, row_frac, col_pos, col_frac, col_band)
    return out[None, :2], out[2]


def solution(mesh):
    placed = (
        P(("parts", "date"), None, None, None),
        P(None, "parts", "date"),
        P("date"),
        P("date"),
        P(("parts", "date"), None),
        P(("parts", "date"), None),
        P(("parts", "date"), None),
        P(("parts", "date"), None),
        P(("parts", "date"), None),
        P(("parts", "date"), None),
    )
    return jax.shard_map(
        functools.partial(per_device, mesh.shape["date"]),
        mesh=mesh,
        in_specs=placed,
        out_specs=(P(("parts", "date"), None, None, None), P("parts", None)),
        check_vma=False,
    )
```

```python
import functools
import math

import jax
import jax.numpy as jnp
from jax import lax
from jax.experimental import pallas as pl
from jax.experimental.pallas import tpu as pltpu
from jax.sharding import PartitionSpec as P

TAPS = 8
LEAD = TAPS // 2 - 1
BLK = 128
WIN = 192
LOOK_AZ = 4
LOOK_RG = 16
HALF = 64
EPSILON = 1e-06
MESH = pl.DeviceIdType.MESH
SIN_TERMS = (4.442882919124343, -7.308245686509025, 3.6063542184321515, -0.8461116503693629, 0.10982451641673696)
COS_TERMS = (1.414213496255228, -6.978850948563791, 5.739460376906791, -1.8835579059844396, 0.3106880275224321)


def poly(terms, x):
    total = jnp.full_like(x, terms[-1])
    for term in terms[-2::-1]:
        total = total * x + term
    return total


def sincos_turns(turns):
    rest = turns - jnp.round(turns)
    square = rest * rest
    sine = rest * poly(SIN_TERMS, square)
    cosine = poly(COS_TERMS, square)
    return sine * cosine, 1.0 - sine * sine


def tap_weights(fraction):
    step = lax.broadcasted_iota(jnp.int32, (TAPS, fraction.shape[1]), 0) - LEAD
    spacing = step.astype(jnp.float32) - fraction
    angle = math.pi * spacing
    sine, _ = sincos_turns(spacing * 0.5)
    sinc = jnp.where(spacing == 0.0, 1.0, sine / jnp.where(spacing == 0.0, 1.0, angle))
    _, cosine = sincos_turns(spacing * 0.125)
    return sinc * (0.5 + 0.5 * cosine)


def tap_matrix(first, weights, cells):
    cell = lax.broadcasted_iota(jnp.int32, (cells, first.shape[1]), 0) - first
    total = jnp.zeros(cell.shape, jnp.float32)
    for k in range(TAPS):
        total = jnp.where(cell == k, weights[k : k + 1], total)
    return total.astype(jnp.bfloat16)


def slab_sum(values):
    rows = values.shape[0] // LOOK_AZ
    total = values[:rows]
    for b in range(1, LOOK_AZ):
        total = total + values[b * rows : (b + 1) * rows]
    return total


def halves(values):
    high = values.astype(jnp.bfloat16)
    low = (values - high.astype(jnp.float32)).astype(jnp.bfloat16)
    return jnp.concatenate([high, low], axis=1)


def looked(rows, gather, shift):
    count, height, width = rows.shape
    sums = jnp.dot(rows.reshape(count * height, width), gather, preferred_element_type=jnp.float32)
    total = sums[:height]
    for b in range(1, count):
        total = total + pltpu.roll(sums[b * height : (b + 1) * height], b * shift, 1)
    return total


def kernel(
    parties,
    x_hbm, master_hbm, rate_hbm, center_hbm, row_pos_hbm, row_frac_hbm, col_pos_hbm, col_frac_hbm, col_band_hbm,
    ifg_ref, stack_ref,
    master_ref, rate_ref, center_ref, row_pos, row_frac, col_pos, col_frac, col_band,
    x0, xs, weights, own_rc, rc, mg, res, times, place, rows_all, sec_rows, sec, outgoing, powers,
    small_sems, in_sems, rc_s, rc_r, m_s, m_r, p_s, p_r,
):
    me = lax.axis_index("date")
    deep = parties // 4
    my_z, my_y, my_c = me // 4, (me // 2) % 2, me % 2
    across = my_z * 4 + (1 - my_y) * 2 + my_c
    twin = my_z * 4 + my_y * 2 + (1 - my_c)
    lines_in = x0.shape[1]
    tiles_in = xs.shape[0] // 2
    last_half = xs.shape[0] - 3
    blocks = col_pos.shape[1] // BLK
    rows_out = row_pos.shape[1]
    looks_out = rows_out // LOOK_AZ
    shift = BLK // LOOK_RG
    per_tile = BLK // shift
    per_part = per_tile // 2
    part_steps = per_part // 4

    small = [
        pltpu.make_async_copy(source, target, small_sems.at[i])
        for i, (source, target) in enumerate((
            (master_hbm, master_ref), (rate_hbm, rate_ref), (center_hbm, center_ref), (col_frac_hbm, col_frac),
            (row_pos_hbm, row_pos), (row_frac_hbm, row_frac), (col_pos_hbm, col_pos), (col_band_hbm, col_band)))
    ]
    for copy in small:
        copy.start()
    fetch0 = pltpu.make_async_copy(x_hbm.at[0], x0, in_sems.at[0])
    fetch0.start()

    def tile_copy(t):
        lanes = pl.ds(pl.multiple_of(t * BLK, BLK), BLK)
        return pltpu.make_async_copy(x_hbm.at[0, :, :, lanes], xs.at[2 * t], in_sems.at[t + 1])

    def tile_start(t, _):
        tile_copy(t).start()
        return 0

    def tile_wait(t, _):
        tile_copy(t).wait()
        return 0

    lax.fori_loop(0, tiles_in, tile_start, 0)

    barrier = pltpu.get_barrier_semaphore()

    def greet(s, _):
        pl.semaphore_signal(barrier, inc=1, device_id={"date": lax.rem(me + s, parties)}, device_id_type=MESH)
        return 0

    lax.fori_loop(1, parties, greet, 0)

    for copy in small[:3]:
        copy.wait()

    own_rc[...] = jnp.zeros_like(own_rc)
    own_rc[0:1, :] = rate_ref[...] * (0.5 / math.pi)
    own_rc[1:2, :] = center_ref[...]
    rc[pl.ds(me, 1)] = own_rc[...][None]
    to = lax.broadcasted_iota(jnp.int32, (rows_out, rows_out), 0)
    source = lax.broadcasted_iota(jnp.int32, (rows_out, rows_out), 1)
    order = jnp.where(source == LOOK_AZ * (to % looks_out) + to // looks_out, 1.0, 0.0).astype(jnp.bfloat16)
    for p in range(2):
        mg[pl.ds(me, 1), p] = jnp.dot(order, master_ref[p], preferred_element_type=jnp.float32).astype(jnp.bfloat16)[None]

    pl.semaphore_wait(barrier, parties - 1)

    def rc_copy(slot, peer):
        return pltpu.make_async_remote_copy(
            src_ref=own_rc, dst_ref=rc.at[slot], send_sem=rc_s, recv_sem=rc_r,
            device_id={"date": peer}, device_id_type=MESH)

    def rc_all():
        every = rc.at[pl.ds(0, parties - 1)]
        return pltpu.make_async_remote_copy(
            src_ref=every, dst_ref=every, send_sem=rc_s, recv_sem=rc_r,
            device_id={"date": twin}, device_id_type=MESH)

    def rc_send(s, _):
        rc_copy(me, lax.rem(me + s, parties)).start()
        return 0

    lax.fori_loop(1, parties, rc_send, 0)


    def m_copy(slot, peer, kind, tag):
        return pltpu.make_async_remote_copy(
            src_ref=mg.at[slot], dst_ref=mg.at[slot], send_sem=m_s.at[kind, tag], recv_sem=m_r.at[slot],
            device_id={"date": peer}, device_id_type=MESH)

    def z_index(s):
        return lax.rem(my_z + s, deep) * 4

    def z_send(s, _):
        peer = z_index(s) + my_y * 2 + my_c
        m_copy(me, peer, 0, peer).start()
        return 0

    m_copy(me, across, 1, me).start()
    lax.fori_loop(1, deep, z_send, 0)
    m_copy(me, twin, 2, me).start()

    def z_pass(s, _):
        slot = z_index(s) + my_y * 2 + my_c
        m_copy(slot, slot, 0, slot).wait_recv()
        m_copy(slot, across, 1, slot).start()
        m_copy(slot, twin, 2, slot).start()
        return 0

    def y_pass(s, _):
        slot = z_index(s) + (1 - my_y) * 2 + my_c
        m_copy(slot, across, 1, slot).wait_recv()
        m_copy(slot, twin, 2, slot).start()
        return 0

    def twin_wait(y):
        def wait(s, _):
            slot = z_index(s) + y * 2 + (1 - my_c)
            m_copy(slot, twin, 2, slot).wait_recv()
            return 0

        lax.fori_loop(0, deep, wait, 0)

    for copy in small[3:]:
        copy.wait()

    weights[...] = tap_weights(col_frac[...])
    row_taps = tap_matrix(row_pos[...] - LEAD, tap_weights(row_frac[...]), lines_in)
    row_taps = lax.dot_general(
        order, row_taps, (((1,), (1,)), ((), ())), preferred_element_type=jnp.float32
    ).astype(jnp.bfloat16)
    when = (row_pos[...].astype(jnp.float32) + row_frac[...]) / lines_in
    times[...] = jnp.transpose(jnp.broadcast_to(when, (BLK, rows_out)))
    for b in range(LOOK_AZ):
        place[b * looks_out : (b + 1) * looks_out, :] = times[pl.ds(b, looks_out, stride=LOOK_AZ), :]
    lane = lax.broadcasted_iota(jnp.int32, (2 * BLK, BLK), 0) % BLK
    out_lane = lax.broadcasted_iota(jnp.int32, (2 * BLK, BLK), 1)
    gather = jnp.where(lane // LOOK_RG == out_lane, 1.0, 0.0).astype(jnp.bfloat16)

    fetch0.wait()
    lax.fori_loop(0, tiles_in, tile_wait, 0)
    for t in range(tiles_in):
        xs[2 * t + 1] = x0[:, :, t * BLK + HALF : (t + 1) * BLK + HALF]

    rc_all().wait_recv()

    line_time = lax.broadcasted_iota(jnp.int32, (lines_in, BLK), 0).astype(jnp.float32) / lines_in

    def resample(b):
        half = lax.min(lax.div(col_band[0, b], HALF), last_half)
        window = jnp.concatenate([xs[half], xs[half + 2]], axis=2).reshape(2 * lines_in, 2 * BLK)
        columns = pl.ds(pl.multiple_of(b * BLK, BLK), BLK)
        taps = tap_matrix(col_pos[:, columns] - (LEAD + HALF * half), weights[:, columns], 2 * BLK)
        ranged = jnp.dot(window, taps, preferred_element_type=jnp.float32)
        rate, center = rc[b, 0:1, :], rc[b, 1:2, :]
        offset = line_time - center
        sine, cosine = sincos_turns(rate * offset * offset)
        real, imag = ranged[:lines_in], ranged[lines_in:]
        deramped = jnp.concatenate(
            [(real * cosine + imag * sine).astype(jnp.bfloat16), (imag * cosine - real * sine).astype(jnp.bfloat16)],
            axis=1)
        moved = jnp.dot(row_taps, deramped, preferred_element_type=jnp.float32)
        offset = place[...] - center
        sine, cosine = sincos_turns(rate * offset * offset)
        real, imag = moved[:, :BLK], moved[:, BLK:]
        real, imag = (
            (real * cosine - imag * sine).astype(jnp.bfloat16),
            (real * sine + imag * cosine).astype(jnp.bfloat16),
        )
        res[b, 0] = real
        res[b, 1] = imag
        real, imag = real.astype(jnp.float32), imag.astype(jnp.float32)
        sec_rows[b] = halves(slab_sum(real * real + imag * imag))

    def p_copy(part, peer):
        return pltpu.make_async_remote_copy(
            src_ref=outgoing.at[part], dst_ref=powers.at[part, me], send_sem=p_s.at[part], recv_sem=p_r.at[part],
            device_id={"date": peer}, device_id_type=MESH)

    def p_all(part):
        every = powers.at[part, pl.ds(0, parties - 1)]
        return pltpu.make_async_remote_copy(
            src_ref=every, dst_ref=every, send_sem=p_s.at[part], recv_sem=p_r.at[part],
            device_id={"date": twin}, device_id_type=MESH)

    def step(i, _):
        for q in range(4):
            resample(4 * i + q)

        @pl.when(i == 1)
        def _():
            lax.fori_loop(1, deep, z_pass, 0)

        @pl.when(i % part_steps == part_steps - 1)
        def _():
            part = i // part_steps
            here = looked(sec_rows[pl.ds(part * per_part, per_part)], gather, shift)
            sec[part] = here
            packed = here[: looks_out // 2] + pltpu.roll(here[looks_out // 2 :], BLK // 2, 1)
            packed = packed.astype(jnp.bfloat16)
            outgoing[part] = packed
            powers[part, pl.ds(me, 1)] = packed[None]

            def p_send(s, _):
                p_copy(part, lax.rem(me + s, parties)).start()
                return 0

            lax.fori_loop(1, parties, p_send, 0)

        return 0

    lax.fori_loop(0, blocks // 4, step, 0)
    def combine(b):
        m0, m1 = mg[b, 0].astype(jnp.float32), mg[b, 1].astype(jnp.float32)
        r0, r1 = res[b, 0].astype(jnp.float32), res[b, 1].astype(jnp.float32)
        rows = jnp.concatenate(
            [slab_sum(m0 * r0 + m1 * r1), slab_sum(m1 * r0 - m0 * r1), slab_sum(m0 * m0 + m1 * m1)], axis=0)
        rows_all[b] = halves(rows)

    def combine_some(y, c):
        def combine_step(i, _):
            combine(8 * i + 2 * y + c)
            combine(8 * i + 4 + 2 * y + c)
            return 0

        lax.fori_loop(0, deep // 2, combine_step, 0)

    combine_some(my_y, my_c)
    twin_wait(my_y)
    lax.fori_loop(0, deep, y_pass, 0)
    combine_some(my_y, 1 - my_c)
    combine_some(1 - my_y, my_c)
    twin_wait(1 - my_y)
    combine_some(1 - my_y, 1 - my_c)

    scale = 1.0 / (LOOK_AZ * LOOK_RG)
    left = lax.broadcasted_iota(jnp.int32, (looks_out // 2, BLK), 1) < BLK // 2
    for t in range(blocks // per_tile):
        lanes = slice(t * BLK, (t + 1) * BLK)
        sums = looked(rows_all[t * per_tile : (t + 1) * per_tile], gather, shift) * scale
        real, imag, ref = (sums[q * looks_out : (q + 1) * looks_out] for q in range(3))
        mine = (sec[2 * t] + pltpu.roll(sec[2 * t + 1], BLK // 2, 1)) * scale
        normalizer = 1.0 / jnp.sqrt(ref * mine + EPSILON)
        ifg_ref[0, :, lanes] = real * normalizer
        ifg_ref[1, :, lanes] = imag * normalizer
    for t in range(blocks // per_tile):
        lanes = slice(t * BLK, (t + 1) * BLK)
        p_all(2 * t).wait_recv()
        p_all(2 * t + 1).wait_recv()
        first, second = (
            jnp.sum(powers[2 * t + q].astype(jnp.float32), axis=0) * (scale / parties) for q in range(2))
        stack_ref[: looks_out // 2, lanes] = jnp.where(left, first, pltpu.roll(second, BLK // 2, 1))
        stack_ref[looks_out // 2 :, lanes] = jnp.where(left, pltpu.roll(first, BLK // 2, 1), second)

    rc_all().wait_send()
    for part in range(blocks // per_part):
        p_all(part).wait_send()

    def z_sent(s, _):
        peer = z_index(s) + my_y * 2 + my_c
        m_copy(me, peer, 0, peer).wait_send()
        return 0

    def forward_sent(s, _):
        near = z_index(s) + my_y * 2 + my_c
        far = z_index(s) + (1 - my_y) * 2 + my_c
        m_copy(near, across, 1, near).wait_send()
        m_copy(near, twin, 2, near).wait_send()
        m_copy(far, twin, 2, far).wait_send()
        return 0

    lax.fori_loop(1, deep, z_sent, 0)
    lax.fori_loop(0, deep, forward_sent, 0)


def per_device(
    parties, x, master, rate, center, row_pos, row_frac, row_band, col_pos, col_frac, col_band,
):
    lines_in, cells = x.shape[2], x.shape[3]
    samples = col_pos.shape[1]
    rows_out = row_pos.shape[1]
    blocks = samples // BLK
    looks_out, look_lanes = rows_out // LOOK_AZ, samples // LOOK_RG
    tiles = -(-look_lanes // BLK)
    tiles_in = (cells - HALF) // BLK
    vmem = pl.BlockSpec(memory_space=pltpu.VMEM)
    dma = pltpu.SemaphoreType.DMA
    f32, bf16 = jnp.float32, jnp.bfloat16
    ifg, stack = pl.pallas_call(
        functools.partial(kernel, parties),
        out_shape=(
            jax.ShapeDtypeStruct((2, looks_out, look_lanes), f32),
            jax.ShapeDtypeStruct((looks_out, look_lanes), f32),
        ),
        in_specs=[pl.BlockSpec(memory_space=pl.ANY)] * 9,
        out_specs=(vmem, vmem),
        scratch_shapes=[
            pltpu.VMEM(master.shape, bf16),
            pltpu.VMEM((1, BLK), f32),
            pltpu.VMEM((1, BLK), f32),
            pltpu.VMEM(row_pos.shape, jnp.int32),
            pltpu.VMEM(row_frac.shape, f32),
            pltpu.VMEM(col_pos.shape, jnp.int32),
            pltpu.VMEM(col_frac.shape, f32),
            pltpu.SMEM(col_band.shape, jnp.int32),
            pltpu.VMEM((2, lines_in, cells), bf16),
            pltpu.VMEM((2 * tiles_in, 2, lines_in, BLK), bf16),
            pltpu.VMEM((TAPS, samples), f32),
            pltpu.VMEM((8, BLK), f32),
            pltpu.VMEM((parties, 8, BLK), f32),
            pltpu.VMEM((parties, 2, rows_out, BLK), bf16),
            pltpu.VMEM((blocks, 2, rows_out, BLK), bf16),
            pltpu.VMEM((rows_out, BLK), f32),
            pltpu.VMEM((rows_out, BLK), f32),
            pltpu.VMEM((blocks, 3 * looks_out, 2 * BLK), bf16),
            pltpu.VMEM((blocks, looks_out, 2 * BLK), bf16),
            pltpu.VMEM((2 * tiles, looks_out, BLK), f32),
            pltpu.VMEM((2 * tiles, looks_out // 2, BLK), bf16),
            pltpu.VMEM((2 * tiles, parties, looks_out // 2, BLK), bf16),
            dma((8,)),
            dma((tiles_in + 1,)),
            dma, dma,
            dma((3, parties)), dma((parties,)),
            dma((2 * tiles,)), dma((2 * tiles,)),
        ],
        compiler_params=pltpu.CompilerParams(
            collective_id=0, has_side_effects=True, vmem_limit_bytes=60 * 1024 * 1024
        ),
        cost_estimate=pl.CostEstimate(flops=6 * 10**8, bytes_accessed=4 * 10**6, transcendentals=0),
        name="coregister",
    )(x, master, rate[None], center[None], row_pos, row_frac, col_pos, col_frac, col_band)
    return ifg[None], stack


def solution(mesh):
    placed = (
        P(("parts", "date"), None, None, None),
        P(None, "parts", "date"),
        P("date"),
        P("date"),
        P(("parts", "date"), None),
        P(("parts", "date"), None),
        P(("parts", "date"), None),
        P(("parts", "date"), None),
        P(("parts", "date"), None),
        P(("parts", "date"), None),
    )
    return jax.shard_map(
        functools.partial(per_device, mesh.shape["date"]),
        mesh=mesh,
        in_specs=placed,
        out_specs=(P(("parts", "date"), None, None, None), P("parts", None)),
        check_vma=False,
    )
```

```python
import functools
import math

import jax
import jax.numpy as jnp
from jax import lax
from jax.experimental import pallas as pl
from jax.experimental.pallas import tpu as pltpu
from jax.sharding import PartitionSpec as P

TAPS = 8
LEAD = TAPS // 2 - 1
BLK = 128
WIN = 192
LOOK_AZ = 4
LOOK_RG = 16
HALF = 64
EPSILON = 1e-06
MESH = pl.DeviceIdType.MESH
SIN_TERMS = (4.442882919124343, -7.308245686509025, 3.6063542184321515, -0.8461116503693629, 0.10982451641673696)
COS_TERMS = (1.414213496255228, -6.978850948563791, 5.739460376906791, -1.8835579059844396, 0.3106880275224321)


def poly(terms, x):
    total = jnp.full_like(x, terms[-1])
    for term in terms[-2::-1]:
        total = total * x + term
    return total


def sincos_turns(turns):
    rest = turns - jnp.round(turns)
    square = rest * rest
    sine = rest * poly(SIN_TERMS, square)
    cosine = poly(COS_TERMS, square)
    return sine * cosine, 1.0 - sine * sine


def tap_weights(fraction):
    step = lax.broadcasted_iota(jnp.int32, (TAPS, fraction.shape[1]), 0) - LEAD
    spacing = step.astype(jnp.float32) - fraction
    angle = math.pi * spacing
    sine, _ = sincos_turns(spacing * 0.5)
    sinc = jnp.where(spacing == 0.0, 1.0, sine / jnp.where(spacing == 0.0, 1.0, angle))
    _, cosine = sincos_turns(spacing * 0.125)
    return sinc * (0.5 + 0.5 * cosine)


def tap_matrix(first, weights, cells):
    cell = lax.broadcasted_iota(jnp.int32, (cells, first.shape[1]), 0) - first
    total = jnp.zeros(cell.shape, jnp.float32)
    for k in range(TAPS):
        total = jnp.where(cell == k, weights[k : k + 1], total)
    return total.astype(jnp.bfloat16)


def slab_sum(values):
    rows = values.shape[0] // LOOK_AZ
    total = values[:rows]
    for b in range(1, LOOK_AZ):
        total = total + values[b * rows : (b + 1) * rows]
    return total


def halves(values):
    high = values.astype(jnp.bfloat16)
    low = (values - high.astype(jnp.float32)).astype(jnp.bfloat16)
    return jnp.concatenate([high, low], axis=1)


def looked(rows, gather, shift):
    count, height, width = rows.shape
    sums = jnp.dot(rows.reshape(count * height, width), gather, preferred_element_type=jnp.float32)
    total = sums[:height]
    for b in range(1, count):
        total = total + pltpu.roll(sums[b * height : (b + 1) * height], b * shift, 1)
    return total


def kernel(
    parties,
    x_hbm, master_hbm, rate_hbm, center_hbm, row_pos_hbm, row_frac_hbm, col_pos_hbm, col_frac_hbm, col_band_hbm,
    ifg_ref, stack_ref,
    master_ref, rate_ref, center_ref, row_pos, row_frac, col_pos, col_frac, col_band,
    x0, xs, weights, own_rc, rc, mg, res, times, place, rows_all, sec_rows, sec, outgoing, powers,
    small_sems, in_sems, rc_s, rc_r, m_s, m_r, p_s, p_r,
):
    me = lax.axis_index("date")
    deep = parties // 4
    my_z, my_y, my_c = me // 4, (me // 2) % 2, me % 2
    across = my_z * 4 + (1 - my_y) * 2 + my_c
    twin = my_z * 4 + my_y * 2 + (1 - my_c)
    lines_in = x0.shape[1]
    tiles_in = xs.shape[0] // 2
    last_half = xs.shape[0] - 3
    blocks = col_pos.shape[1] // BLK
    rows_out = row_pos.shape[1]
    looks_out = rows_out // LOOK_AZ
    shift = BLK // LOOK_RG
    per_tile = BLK // shift
    per_part = per_tile // 2
    part_steps = per_part // 2

    barrier = pltpu.get_barrier_semaphore()

    def greet(s, _):
        pl.semaphore_signal(barrier, inc=1, device_id={"date": lax.rem(me + s, parties)}, device_id_type=MESH)
        return 0

    lax.fori_loop(1, parties, greet, 0)

    small = [
        pltpu.make_async_copy(source, target, small_sems.at[i])
        for i, (source, target) in enumerate((
            (master_hbm, master_ref), (rate_hbm, rate_ref), (center_hbm, center_ref), (col_frac_hbm, col_frac),
            (row_pos_hbm, row_pos), (row_frac_hbm, row_frac), (col_pos_hbm, col_pos), (col_band_hbm, col_band)))
    ]
    for copy in small:
        copy.start()
    fetch0 = pltpu.make_async_copy(x_hbm.at[0], x0, in_sems.at[0])
    fetch0.start()

    def tile_copy(t):
        lanes = pl.ds(pl.multiple_of(t * BLK, BLK), BLK)
        return pltpu.make_async_copy(x_hbm.at[0, :, :, lanes], xs.at[2 * t], in_sems.at[t + 1])

    def tile_start(t, _):
        tile_copy(t).start()
        return 0

    def tile_wait(t, _):
        tile_copy(t).wait()
        return 0

    lax.fori_loop(0, tiles_in, tile_start, 0)

    for copy in small[:3]:
        copy.wait()

    own_rc[...] = jnp.zeros_like(own_rc)
    own_rc[0:1, :] = rate_ref[...] * (0.5 / math.pi)
    own_rc[1:2, :] = center_ref[...]
    rc[pl.ds(me, 1)] = own_rc[...][None]
    to = lax.broadcasted_iota(jnp.int32, (rows_out, rows_out), 0)
    source = lax.broadcasted_iota(jnp.int32, (rows_out, rows_out), 1)
    order = jnp.where(source == LOOK_AZ * (to % looks_out) + to // looks_out, 1.0, 0.0).astype(jnp.bfloat16)
    for p in range(2):
        mg[pl.ds(me, 1), p] = jnp.dot(order, master_ref[p], preferred_element_type=jnp.float32).astype(jnp.bfloat16)[None]

    pl.semaphore_wait(barrier, parties - 1)

    def rc_copy(slot, peer):
        return pltpu.make_async_remote_copy(
            src_ref=own_rc, dst_ref=rc.at[slot], send_sem=rc_s, recv_sem=rc_r,
            device_id={"date": peer}, device_id_type=MESH)

    def rc_all():
        every = rc.at[pl.ds(0, parties - 1)]
        return pltpu.make_async_remote_copy(
            src_ref=every, dst_ref=every, send_sem=rc_s, recv_sem=rc_r,
            device_id={"date": twin}, device_id_type=MESH)

    def rc_send(s, _):
        rc_copy(me, lax.rem(me + s, parties)).start()
        return 0

    lax.fori_loop(1, parties, rc_send, 0)


    def m_copy(slot, peer, kind, tag):
        return pltpu.make_async_remote_copy(
            src_ref=mg.at[slot], dst_ref=mg.at[slot], send_sem=m_s.at[kind, tag], recv_sem=m_r.at[slot],
            device_id={"date": peer}, device_id_type=MESH)

    def z_index(s):
        return lax.rem(my_z + s, deep) * 4

    def z_send(s, _):
        peer = z_index(s) + my_y * 2 + my_c
        m_copy(me, peer, 0, peer).start()
        return 0

    m_copy(me, across, 1, me).start()
    lax.fori_loop(1, deep, z_send, 0)
    m_copy(me, twin, 2, me).start()

    def z_pass(s, _):
        slot = z_index(s) + my_y * 2 + my_c
        m_copy(slot, slot, 0, slot).wait_recv()
        m_copy(slot, across, 1, slot).start()
        m_copy(slot, twin, 2, slot).start()
        return 0

    def y_pass(s, _):
        slot = z_index(s) + (1 - my_y) * 2 + my_c
        m_copy(slot, across, 1, slot).wait_recv()
        m_copy(slot, twin, 2, slot).start()
        return 0

    def twin_wait(y):
        def wait(s, _):
            slot = z_index(s) + y * 2 + (1 - my_c)
            m_copy(slot, twin, 2, slot).wait_recv()
            return 0

        lax.fori_loop(0, deep, wait, 0)

    for copy in small[3:]:
        copy.wait()

    weights[...] = tap_weights(col_frac[...])
    row_taps = tap_matrix(row_pos[...] - LEAD, tap_weights(row_frac[...]), lines_in)
    row_taps = lax.dot_general(
        order, row_taps, (((1,), (1,)), ((), ())), preferred_element_type=jnp.float32
    ).astype(jnp.bfloat16)
    when = (row_pos[...].astype(jnp.float32) + row_frac[...]) / lines_in
    times[...] = jnp.transpose(jnp.broadcast_to(when, (BLK, rows_out)))
    for b in range(LOOK_AZ):
        place[b * looks_out : (b + 1) * looks_out, :] = times[pl.ds(b, looks_out, stride=LOOK_AZ), :]
    lane = lax.broadcasted_iota(jnp.int32, (2 * BLK, BLK), 0) % BLK
    out_lane = lax.broadcasted_iota(jnp.int32, (2 * BLK, BLK), 1)
    gather = jnp.where(lane // LOOK_RG == out_lane, 1.0, 0.0).astype(jnp.bfloat16)

    fetch0.wait()
    lax.fori_loop(0, tiles_in, tile_wait, 0)
    for t in range(tiles_in):
        xs[2 * t + 1] = x0[:, :, t * BLK + HALF : (t + 1) * BLK + HALF]

    rc_all().wait_recv()

    line_time = lax.broadcasted_iota(jnp.int32, (lines_in, BLK), 0).astype(jnp.float32) / lines_in

    def resample(b):
        half = lax.min(lax.div(col_band[0, b], HALF), last_half)
        window = jnp.concatenate([xs[half], xs[half + 2]], axis=2).reshape(2 * lines_in, 2 * BLK)
        columns = pl.ds(pl.multiple_of(b * BLK, BLK), BLK)
        taps = tap_matrix(col_pos[:, columns] - (LEAD + HALF * half), weights[:, columns], 2 * BLK)
        ranged = jnp.dot(window, taps, preferred_element_type=jnp.float32)
        rate, center = rc[b, 0:1, :], rc[b, 1:2, :]
        offset = line_time - center
        sine, cosine = sincos_turns(rate * offset * offset)
        real, imag = ranged[:lines_in], ranged[lines_in:]
        deramped = jnp.concatenate(
            [(real * cosine + imag * sine).astype(jnp.bfloat16), (imag * cosine - real * sine).astype(jnp.bfloat16)],
            axis=1)
        moved = jnp.dot(row_taps, deramped, preferred_element_type=jnp.float32)
        offset = place[...] - center
        sine, cosine = sincos_turns(rate * offset * offset)
        real, imag = moved[:, :BLK], moved[:, BLK:]
        real, imag = (
            (real * cosine - imag * sine).astype(jnp.bfloat16),
            (real * sine + imag * cosine).astype(jnp.bfloat16),
        )
        res[b, 0] = real
        res[b, 1] = imag
        real, imag = real.astype(jnp.float32), imag.astype(jnp.float32)
        sec_rows[b] = halves(slab_sum(real * real + imag * imag))

    def p_copy(part, peer):
        return pltpu.make_async_remote_copy(
            src_ref=outgoing.at[part], dst_ref=powers.at[part, me], send_sem=p_s.at[part], recv_sem=p_r.at[part],
            device_id={"date": peer}, device_id_type=MESH)

    def p_all(part):
        every = powers.at[part, pl.ds(0, parties - 1)]
        return pltpu.make_async_remote_copy(
            src_ref=every, dst_ref=every, send_sem=p_s.at[part], recv_sem=p_r.at[part],
            device_id={"date": twin}, device_id_type=MESH)

    def step(i, _):
        resample(2 * i)
        resample(2 * i + 1)

        @pl.when(i == 1)
        def _():
            lax.fori_loop(0, 1, y_pass, 0)

        @pl.when(i == 2)
        def _():
            lax.fori_loop(1, 2, z_pass, 0)

        @pl.when(i == 3)
        def _():
            lax.fori_loop(2, deep, z_pass, 0)


        @pl.when(i % part_steps == part_steps - 1)
        def _():
            part = i // part_steps
            here = looked(sec_rows[pl.ds(part * per_part, per_part)], gather, shift)
            sec[part] = here
            packed = here[: looks_out // 2] + pltpu.roll(here[looks_out // 2 :], BLK // 2, 1)
            packed = packed.astype(jnp.bfloat16)
            outgoing[part] = packed
            powers[part, pl.ds(me, 1)] = packed[None]

            def p_send(s, _):
                p_copy(part, lax.rem(me + s, parties)).start()
                return 0

            lax.fori_loop(1, parties, p_send, 0)

        return 0

    lax.fori_loop(0, blocks // 2, step, 0)
    def combine(b):
        m0, m1 = mg[b, 0].astype(jnp.float32), mg[b, 1].astype(jnp.float32)
        r0, r1 = res[b, 0].astype(jnp.float32), res[b, 1].astype(jnp.float32)
        rows = jnp.concatenate(
            [slab_sum(m0 * r0 + m1 * r1), slab_sum(m1 * r0 - m0 * r1), slab_sum(m0 * m0 + m1 * m1)], axis=0)
        rows_all[b] = halves(rows)

    def combine_some(y, c):
        def combine_step(i, _):
            combine(8 * i + 2 * y + c)
            combine(8 * i + 4 + 2 * y + c)
            return 0

        lax.fori_loop(0, deep // 2, combine_step, 0)

    combine_some(my_y, my_c)
    twin_wait(my_y)
    lax.fori_loop(1, deep, y_pass, 0)
    combine_some(my_y, 1 - my_c)
    combine_some(1 - my_y, my_c)
    twin_wait(1 - my_y)
    combine_some(1 - my_y, 1 - my_c)

    scale = 1.0 / (LOOK_AZ * LOOK_RG)
    left = lax.broadcasted_iota(jnp.int32, (looks_out // 2, BLK), 1) < BLK // 2
    for t in range(blocks // per_tile):
        lanes = slice(t * BLK, (t + 1) * BLK)
        sums = looked(rows_all[t * per_tile : (t + 1) * per_tile], gather, shift) * scale
        real, imag, ref = (sums[q * looks_out : (q + 1) * looks_out] for q in range(3))
        mine = (sec[2 * t] + pltpu.roll(sec[2 * t + 1], BLK // 2, 1)) * scale
        normalizer = 1.0 / jnp.sqrt(ref * mine + EPSILON)
        ifg_ref[0, :, lanes] = real * normalizer
        ifg_ref[1, :, lanes] = imag * normalizer
    for t in range(blocks // per_tile):
        lanes = slice(t * BLK, (t + 1) * BLK)
        p_all(2 * t).wait_recv()
        p_all(2 * t + 1).wait_recv()
        first, second = (
            jnp.sum(powers[2 * t + q].astype(jnp.float32), axis=0) * (scale / parties) for q in range(2))
        stack_ref[: looks_out // 2, lanes] = jnp.where(left, first, pltpu.roll(second, BLK // 2, 1))
        stack_ref[looks_out // 2 :, lanes] = jnp.where(left, pltpu.roll(first, BLK // 2, 1), second)

    rc_all().wait_send()
    for part in range(blocks // per_part):
        p_all(part).wait_send()

    def z_sent(s, _):
        peer = z_index(s) + my_y * 2 + my_c
        m_copy(me, peer, 0, peer).wait_send()
        return 0

    def forward_sent(s, _):
        near = z_index(s) + my_y * 2 + my_c
        far = z_index(s) + (1 - my_y) * 2 + my_c
        m_copy(near, across, 1, near).wait_send()
        m_copy(near, twin, 2, near).wait_send()
        m_copy(far, twin, 2, far).wait_send()
        return 0

    lax.fori_loop(1, deep, z_sent, 0)
    lax.fori_loop(0, deep, forward_sent, 0)


def per_device(
    parties, x, master, rate, center, row_pos, row_frac, row_band, col_pos, col_frac, col_band,
):
    lines_in, cells = x.shape[2], x.shape[3]
    samples = col_pos.shape[1]
    rows_out = row_pos.shape[1]
    blocks = samples // BLK
    looks_out, look_lanes = rows_out // LOOK_AZ, samples // LOOK_RG
    tiles = -(-look_lanes // BLK)
    tiles_in = (cells - HALF) // BLK
    vmem = pl.BlockSpec(memory_space=pltpu.VMEM)
    dma = pltpu.SemaphoreType.DMA
    f32, bf16 = jnp.float32, jnp.bfloat16
    ifg, stack = pl.pallas_call(
        functools.partial(kernel, parties),
        out_shape=(
            jax.ShapeDtypeStruct((2, looks_out, look_lanes), f32),
            jax.ShapeDtypeStruct((looks_out, look_lanes), f32),
        ),
        in_specs=[pl.BlockSpec(memory_space=pl.ANY)] * 9,
        out_specs=(vmem, vmem),
        scratch_shapes=[
            pltpu.VMEM(master.shape, bf16),
            pltpu.VMEM((1, BLK), f32),
            pltpu.VMEM((1, BLK), f32),
            pltpu.VMEM(row_pos.shape, jnp.int32),
            pltpu.VMEM(row_frac.shape, f32),
            pltpu.VMEM(col_pos.shape, jnp.int32),
            pltpu.VMEM(col_frac.shape, f32),
            pltpu.SMEM(col_band.shape, jnp.int32),
            pltpu.VMEM((2, lines_in, cells), bf16),
            pltpu.VMEM((2 * tiles_in, 2, lines_in, BLK), bf16),
            pltpu.VMEM((TAPS, samples), f32),
            pltpu.VMEM((8, BLK), f32),
            pltpu.VMEM((parties, 8, BLK), f32),
            pltpu.VMEM((parties, 2, rows_out, BLK), bf16),
            pltpu.VMEM((blocks, 2, rows_out, BLK), bf16),
            pltpu.VMEM((rows_out, BLK), f32),
            pltpu.VMEM((rows_out, BLK), f32),
            pltpu.VMEM((blocks, 3 * looks_out, 2 * BLK), bf16),
            pltpu.VMEM((blocks, looks_out, 2 * BLK), bf16),
            pltpu.VMEM((2 * tiles, looks_out, BLK), f32),
            pltpu.VMEM((2 * tiles, looks_out // 2, BLK), bf16),
            pltpu.VMEM((2 * tiles, parties, looks_out // 2, BLK), bf16),
            dma((8,)),
            dma((tiles_in + 1,)),
            dma, dma,
            dma((3, parties)), dma((parties,)),
            dma((2 * tiles,)), dma((2 * tiles,)),
        ],
        compiler_params=pltpu.CompilerParams(
            collective_id=0, has_side_effects=True, vmem_limit_bytes=60 * 1024 * 1024
        ),
        cost_estimate=pl.CostEstimate(flops=6 * 10**8, bytes_accessed=4 * 10**6, transcendentals=0),
        name="coregister",
    )(x, master, rate[None], center[None], row_pos, row_frac, col_pos, col_frac, col_band)
    return ifg[None], stack


def solution(mesh):
    placed = (
        P(("parts", "date"), None, None, None),
        P(None, "parts", "date"),
        P("date"),
        P("date"),
        P(("parts", "date"), None),
        P(("parts", "date"), None),
        P(("parts", "date"), None),
        P(("parts", "date"), None),
        P(("parts", "date"), None),
        P(("parts", "date"), None),
    )
    return jax.shard_map(
        functools.partial(per_device, mesh.shape["date"]),
        mesh=mesh,
        in_specs=placed,
        out_specs=(P(("parts", "date"), None, None, None), P("parts", None)),
        check_vma=False,
    )
```

```python
import functools
import math

import jax
import jax.numpy as jnp
from jax import lax
from jax.experimental import pallas as pl
from jax.experimental.pallas import tpu as pltpu
from jax.sharding import PartitionSpec as P

TAPS = 8
LEAD = TAPS // 2 - 1
BLK = 128
WIN = 192
LOOK_AZ = 4
LOOK_RG = 16
HALF = 64
EPSILON = 1e-06
MESH = pl.DeviceIdType.MESH
SIN_TERMS = (4.442882919124343, -7.308245686509025, 3.6063542184321515, -0.8461116503693629, 0.10982451641673696)
COS_TERMS = (1.414213496255228, -6.978850948563791, 5.739460376906791, -1.8835579059844396, 0.3106880275224321)


def poly(terms, x):
    total = jnp.full_like(x, terms[-1])
    for term in terms[-2::-1]:
        total = total * x + term
    return total


def sincos_turns(turns):
    rest = turns - jnp.round(turns)
    square = rest * rest
    sine = rest * poly(SIN_TERMS, square)
    cosine = poly(COS_TERMS, square)
    return sine * cosine, 1.0 - sine * sine


def tap_weights(fraction):
    step = lax.broadcasted_iota(jnp.int32, (TAPS, fraction.shape[1]), 0) - LEAD
    spacing = step.astype(jnp.float32) - fraction
    angle = math.pi * spacing
    sine, _ = sincos_turns(spacing * 0.5)
    sinc = jnp.where(spacing == 0.0, 1.0, sine / jnp.where(spacing == 0.0, 1.0, angle))
    _, cosine = sincos_turns(spacing * 0.125)
    return sinc * (0.5 + 0.5 * cosine)


def tap_matrix(first, weights, cells):
    cell = lax.broadcasted_iota(jnp.int32, (cells, first.shape[1]), 0) - first
    total = jnp.zeros(cell.shape, jnp.float32)
    for k in range(TAPS):
        total = jnp.where(cell == k, weights[k : k + 1], total)
    return total.astype(jnp.bfloat16)


def slab_sum(values):
    rows = values.shape[0] // LOOK_AZ
    total = values[:rows]
    for b in range(1, LOOK_AZ):
        total = total + values[b * rows : (b + 1) * rows]
    return total


def halves(values):
    high = values.astype(jnp.bfloat16)
    low = (values - high.astype(jnp.float32)).astype(jnp.bfloat16)
    return jnp.concatenate([high, low], axis=1)


def looked(rows, gather, shift):
    count, height, width = rows.shape
    sums = jnp.dot(rows.reshape(count * height, width), gather, preferred_element_type=jnp.float32)
    total = sums[:height]
    for b in range(1, count):
        total = total + pltpu.roll(sums[b * height : (b + 1) * height], b * shift, 1)
    return total


def kernel(
    parties,
    x_hbm, master_hbm, rate_hbm, center_hbm, row_pos_hbm, row_frac_hbm, col_pos_hbm, col_frac_hbm, col_band_hbm,
    ifg_ref, stack_ref,
    master_ref, rate_ref, center_ref, row_pos, row_frac, col_pos, col_frac, col_band,
    x0, xs, weights, own_rc, rc, mg, res, times, place, rows_all, sec_rows, sec, outgoing, powers,
    small_sems, in_sems, rc_s, rc_r, m_s, m_r, p_s, p_r,
):
    me = lax.axis_index("date")
    deep = parties // 4
    my_z, my_y, my_c = me // 4, (me // 2) % 2, me % 2
    across = my_z * 4 + (1 - my_y) * 2 + my_c
    twin = my_z * 4 + my_y * 2 + (1 - my_c)
    lines_in = x0.shape[1]
    tiles_in = xs.shape[0] // 2
    last_half = xs.shape[0] - 3
    blocks = col_pos.shape[1] // BLK
    rows_out = row_pos.shape[1]
    looks_out = rows_out // LOOK_AZ
    shift = BLK // LOOK_RG
    per_tile = BLK // shift
    per_part = per_tile // 2
    part_steps = per_part // 2

    barrier = pltpu.get_barrier_semaphore()

    def greet(s, _):
        pl.semaphore_signal(barrier, inc=1, device_id={"date": lax.rem(me + s, parties)}, device_id_type=MESH)
        return 0

    lax.fori_loop(1, parties, greet, 0)

    small = [
        pltpu.make_async_copy(source, target, small_sems.at[i])
        for i, (source, target) in enumerate((
            (master_hbm, master_ref), (rate_hbm, rate_ref), (center_hbm, center_ref), (col_frac_hbm, col_frac),
            (row_pos_hbm, row_pos), (row_frac_hbm, row_frac), (col_pos_hbm, col_pos), (col_band_hbm, col_band)))
    ]
    for copy in small:
        copy.start()
    fetch0 = pltpu.make_async_copy(x_hbm.at[0], x0, in_sems.at[0])
    fetch0.start()

    def tile_copy(t):
        lanes = pl.ds(pl.multiple_of(t * BLK, BLK), BLK)
        return pltpu.make_async_copy(x_hbm.at[0, :, :, lanes], xs.at[2 * t], in_sems.at[t + 1])

    def tile_start(t, _):
        tile_copy(t).start()
        return 0

    def tile_wait(t, _):
        tile_copy(t).wait()
        return 0

    lax.fori_loop(0, tiles_in, tile_start, 0)

    for copy in small[:3]:
        copy.wait()

    own_rc[...] = jnp.zeros_like(own_rc)
    own_rc[0:1, :] = rate_ref[...] * (0.5 / math.pi)
    own_rc[1:2, :] = center_ref[...]
    rc[pl.ds(me, 1)] = own_rc[...][None]
    to = lax.broadcasted_iota(jnp.int32, (rows_out, rows_out), 0)
    source = lax.broadcasted_iota(jnp.int32, (rows_out, rows_out), 1)
    order = jnp.where(source == LOOK_AZ * (to % looks_out) + to // looks_out, 1.0, 0.0).astype(jnp.bfloat16)
    for p in range(2):
        mg[pl.ds(me, 1), p] = jnp.dot(order, master_ref[p], preferred_element_type=jnp.float32).astype(jnp.bfloat16)[None]

    pl.semaphore_wait(barrier, parties - 1)

    def rc_copy(slot, peer):
        return pltpu.make_async_remote_copy(
            src_ref=own_rc, dst_ref=rc.at[slot], send_sem=rc_s, recv_sem=rc_r,
            device_id={"date": peer}, device_id_type=MESH)

    def rc_all():
        every = rc.at[pl.ds(0, parties - 1)]
        return pltpu.make_async_remote_copy(
            src_ref=every, dst_ref=every, send_sem=rc_s, recv_sem=rc_r,
            device_id={"date": twin}, device_id_type=MESH)

    def rc_send(s, _):
        rc_copy(me, lax.rem(me + s, parties)).start()
        return 0

    lax.fori_loop(1, parties, rc_send, 0)


    def m_copy(slot, peer, kind, tag):
        return pltpu.make_async_remote_copy(
            src_ref=mg.at[slot], dst_ref=mg.at[slot], send_sem=m_s.at[kind], recv_sem=m_r.at[slot],
            device_id={"date": peer}, device_id_type=MESH)

    def z_index(s):
        return lax.rem(my_z + s, deep) * 4

    def z_send(s, _):
        peer = z_index(s) + my_y * 2 + my_c
        m_copy(me, peer, 0, peer).start()
        return 0

    m_copy(me, across, 1, me).start()
    lax.fori_loop(1, deep, z_send, 0)
    m_copy(me, twin, 2, me).start()

    def z_pass(s, _):
        slot = z_index(s) + my_y * 2 + my_c
        m_copy(slot, slot, 0, slot).wait_recv()
        m_copy(slot, across, 1, slot).start()
        m_copy(slot, twin, 2, slot).start()
        return 0

    def y_pass(s, _):
        slot = z_index(s) + (1 - my_y) * 2 + my_c
        m_copy(slot, across, 1, slot).wait_recv()
        m_copy(slot, twin, 2, slot).start()
        return 0

    def twin_wait(y):
        def wait(s, _):
            slot = z_index(s) + y * 2 + (1 - my_c)
            m_copy(slot, twin, 2, slot).wait_recv()
            return 0

        lax.fori_loop(0, deep, wait, 0)

    for copy in small[3:]:
        copy.wait()

    weights[...] = tap_weights(col_frac[...])
    row_taps = tap_matrix(row_pos[...] - LEAD, tap_weights(row_frac[...]), lines_in)
    row_taps = lax.dot_general(
        order, row_taps, (((1,), (1,)), ((), ())), preferred_element_type=jnp.float32
    ).astype(jnp.bfloat16)
    when = (row_pos[...].astype(jnp.float32) + row_frac[...]) / lines_in
    times[...] = jnp.transpose(jnp.broadcast_to(when, (BLK, rows_out)))
    for b in range(LOOK_AZ):
        place[b * looks_out : (b + 1) * looks_out, :] = times[pl.ds(b, looks_out, stride=LOOK_AZ), :]
    lane = lax.broadcasted_iota(jnp.int32, (2 * BLK, BLK), 0) % BLK
    out_lane = lax.broadcasted_iota(jnp.int32, (2 * BLK, BLK), 1)
    gather = jnp.where(lane // LOOK_RG == out_lane, 1.0, 0.0).astype(jnp.bfloat16)

    fetch0.wait()
    lax.fori_loop(0, tiles_in, tile_wait, 0)
    for t in range(tiles_in):
        xs[2 * t + 1] = x0[:, :, t * BLK + HALF : (t + 1) * BLK + HALF]

    rc_all().wait_recv()

    line_time = lax.broadcasted_iota(jnp.int32, (lines_in, BLK), 0).astype(jnp.float32) / lines_in

    def resample(b):
        half = lax.min(lax.div(col_band[0, b], HALF), last_half)
        window = jnp.concatenate([xs[half], xs[half + 2]], axis=2).reshape(2 * lines_in, 2 * BLK)
        columns = pl.ds(pl.multiple_of(b * BLK, BLK), BLK)
        taps = tap_matrix(col_pos[:, columns] - (LEAD + HALF * half), weights[:, columns], 2 * BLK)
        ranged = jnp.dot(window, taps, preferred_element_type=jnp.float32)
        rate, center = rc[b, 0:1, :], rc[b, 1:2, :]
        offset = line_time - center
        sine, cosine = sincos_turns(rate * offset * offset)
        real, imag = ranged[:lines_in], ranged[lines_in:]
        deramped = jnp.concatenate(
            [(real * cosine + imag * sine).astype(jnp.bfloat16), (imag * cosine - real * sine).astype(jnp.bfloat16)],
            axis=1)
        moved = jnp.dot(row_taps, deramped, preferred_element_type=jnp.float32)
        offset = place[...] - center
        sine, cosine = sincos_turns(rate * offset * offset)
        real, imag = moved[:, :BLK], moved[:, BLK:]
        real, imag = (
            (real * cosine - imag * sine).astype(jnp.bfloat16),
            (real * sine + imag * cosine).astype(jnp.bfloat16),
        )
        res[b, 0] = real
        res[b, 1] = imag
        real, imag = real.astype(jnp.float32), imag.astype(jnp.float32)
        sec_rows[b] = halves(slab_sum(real * real + imag * imag))

    def p_copy(part, peer):
        return pltpu.make_async_remote_copy(
            src_ref=outgoing.at[part], dst_ref=powers.at[part, me], send_sem=p_s.at[part], recv_sem=p_r.at[part],
            device_id={"date": peer}, device_id_type=MESH)

    def p_all(part):
        every = powers.at[part, pl.ds(0, parties - 1)]
        return pltpu.make_async_remote_copy(
            src_ref=every, dst_ref=every, send_sem=p_s.at[part], recv_sem=p_r.at[part],
            device_id={"date": twin}, device_id_type=MESH)

    def step(i, _):
        resample(2 * i)
        resample(2 * i + 1)

        @pl.when(i == 1)
        def _():
            lax.fori_loop(0, 1, y_pass, 0)

        @pl.when(i == 2)
        def _():
            lax.fori_loop(1, 2, z_pass, 0)

        @pl.when(i == 3)
        def _():
            lax.fori_loop(2, deep, z_pass, 0)


        @pl.when(i % part_steps == part_steps - 1)
        def _():
            part = i // part_steps
            here = looked(sec_rows[pl.ds(part * per_part, per_part)], gather, shift)
            sec[part] = here
            packed = here[: looks_out // 2] + pltpu.roll(here[looks_out // 2 :], BLK // 2, 1)
            packed = packed.astype(jnp.bfloat16)
            outgoing[part] = packed
            powers[part, pl.ds(me, 1)] = packed[None]

            def p_send(s, _):
                p_copy(part, lax.rem(me + s, parties)).start()
                return 0

            lax.fori_loop(1, parties, p_send, 0)

        return 0

    lax.fori_loop(0, blocks // 2, step, 0)
    def combine(b):
        m0, m1 = mg[b, 0].astype(jnp.float32), mg[b, 1].astype(jnp.float32)
        r0, r1 = res[b, 0].astype(jnp.float32), res[b, 1].astype(jnp.float32)
        rows = jnp.concatenate(
            [slab_sum(m0 * r0 + m1 * r1), slab_sum(m1 * r0 - m0 * r1), slab_sum(m0 * m0 + m1 * m1)], axis=0)
        rows_all[b] = halves(rows)

    def combine_some(y, c):
        def combine_step(i, _):
            combine(8 * i + 2 * y + c)
            combine(8 * i + 4 + 2 * y + c)
            return 0

        lax.fori_loop(0, deep // 2, combine_step, 0)

    combine_some(my_y, my_c)
    twin_wait(my_y)
    lax.fori_loop(1, deep, y_pass, 0)
    combine_some(my_y, 1 - my_c)
    combine_some(1 - my_y, my_c)
    twin_wait(1 - my_y)
    combine_some(1 - my_y, 1 - my_c)

    scale = 1.0 / (LOOK_AZ * LOOK_RG)
    left = lax.broadcasted_iota(jnp.int32, (looks_out // 2, BLK), 1) < BLK // 2
    for t in range(blocks // per_tile):
        lanes = slice(t * BLK, (t + 1) * BLK)
        sums = looked(rows_all[t * per_tile : (t + 1) * per_tile], gather, shift) * scale
        real, imag, ref = (sums[q * looks_out : (q + 1) * looks_out] for q in range(3))
        mine = (sec[2 * t] + pltpu.roll(sec[2 * t + 1], BLK // 2, 1)) * scale
        normalizer = 1.0 / jnp.sqrt(ref * mine + EPSILON)
        ifg_ref[0, :, lanes] = real * normalizer
        ifg_ref[1, :, lanes] = imag * normalizer
    for t in range(blocks // per_tile):
        lanes = slice(t * BLK, (t + 1) * BLK)
        p_all(2 * t).wait_recv()
        p_all(2 * t + 1).wait_recv()
        first, second = (
            jnp.sum(powers[2 * t + q].astype(jnp.float32), axis=0) * (scale / parties) for q in range(2))
        stack_ref[: looks_out // 2, lanes] = jnp.where(left, first, pltpu.roll(second, BLK // 2, 1))
        stack_ref[looks_out // 2 :, lanes] = jnp.where(left, pltpu.roll(first, BLK // 2, 1), second)

    rc_all().wait_send()
    for part in range(blocks // per_part):
        p_all(part).wait_send()

    for kind, count in enumerate((deep - 1, deep, 2 * deep)):
        every = mg.at[pl.ds(0, count)]
        pltpu.make_async_remote_copy(
            src_ref=every, dst_ref=every, send_sem=m_s.at[kind], recv_sem=m_r.at[0],
            device_id={"date": twin}, device_id_type=MESH).wait_send()


def per_device(
    parties, x, master, rate, center, row_pos, row_frac, row_band, col_pos, col_frac, col_band,
):
    lines_in, cells = x.shape[2], x.shape[3]
    samples = col_pos.shape[1]
    rows_out = row_pos.shape[1]
    blocks = samples // BLK
    looks_out, look_lanes = rows_out // LOOK_AZ, samples // LOOK_RG
    tiles = -(-look_lanes // BLK)
    tiles_in = (cells - HALF) // BLK
    vmem = pl.BlockSpec(memory_space=pltpu.VMEM)
    dma = pltpu.SemaphoreType.DMA
    f32, bf16 = jnp.float32, jnp.bfloat16
    ifg, stack = pl.pallas_call(
        functools.partial(kernel, parties),
        out_shape=(
            jax.ShapeDtypeStruct((2, looks_out, look_lanes), f32),
            jax.ShapeDtypeStruct((looks_out, look_lanes), f32),
        ),
        in_specs=[pl.BlockSpec(memory_space=pl.ANY)] * 9,
        out_specs=(vmem, vmem),
        scratch_shapes=[
            pltpu.VMEM(master.shape, bf16),
            pltpu.VMEM((1, BLK), f32),
            pltpu.VMEM((1, BLK), f32),
            pltpu.VMEM(row_pos.shape, jnp.int32),
            pltpu.VMEM(row_frac.shape, f32),
            pltpu.VMEM(col_pos.shape, jnp.int32),
            pltpu.VMEM(col_frac.shape, f32),
            pltpu.SMEM(col_band.shape, jnp.int32),
            pltpu.VMEM((2, lines_in, cells), bf16),
            pltpu.VMEM((2 * tiles_in, 2, lines_in, BLK), bf16),
            pltpu.VMEM((TAPS, samples), f32),
            pltpu.VMEM((8, BLK), f32),
            pltpu.VMEM((parties, 8, BLK), f32),
            pltpu.VMEM((parties, 2, rows_out, BLK), bf16),
            pltpu.VMEM((blocks, 2, rows_out, BLK), bf16),
            pltpu.VMEM((rows_out, BLK), f32),
            pltpu.VMEM((rows_out, BLK), f32),
            pltpu.VMEM((blocks, 3 * looks_out, 2 * BLK), bf16),
            pltpu.VMEM((blocks, looks_out, 2 * BLK), bf16),
            pltpu.VMEM((2 * tiles, looks_out, BLK), f32),
            pltpu.VMEM((2 * tiles, looks_out // 2, BLK), bf16),
            pltpu.VMEM((2 * tiles, parties, looks_out // 2, BLK), bf16),
            dma((8,)),
            dma((tiles_in + 1,)),
            dma, dma,
            dma((3,)), dma((parties,)),
            dma((2 * tiles,)), dma((2 * tiles,)),
        ],
        compiler_params=pltpu.CompilerParams(
            collective_id=0, has_side_effects=True, vmem_limit_bytes=60 * 1024 * 1024
        ),
        cost_estimate=pl.CostEstimate(flops=6 * 10**8, bytes_accessed=4 * 10**6, transcendentals=0),
        name="coregister",
    )(x, master, rate[None], center[None], row_pos, row_frac, col_pos, col_frac, col_band)
    return ifg[None], stack


def solution(mesh):
    placed = (
        P(("parts", "date"), None, None, None),
        P(None, "parts", "date"),
        P("date"),
        P("date"),
        P(("parts", "date"), None),
        P(("parts", "date"), None),
        P(("parts", "date"), None),
        P(("parts", "date"), None),
        P(("parts", "date"), None),
        P(("parts", "date"), None),
    )
    return jax.shard_map(
        functools.partial(per_device, mesh.shape["date"]),
        mesh=mesh,
        in_specs=placed,
        out_specs=(P(("parts", "date"), None, None, None), P("parts", None)),
        check_vma=False,
    )
```
